256 devices in a mesh: frames: 32 (over y_hi, z, core), heads: 8 (over x, y_lo).
Axes of the slice: x: 4, y: 4 (y_hi: 2, y_lo: 2; y = y_hi * 2 + y_lo), z: 8, core: 2. Of those that a mesh axis runs over, the one named last changes fastest.
Arguments:
- tokens: bfloat16 [16384, 1024], P('frames', 'heads'), may hold values from -5 to 5
- norm_gain: float32 [1024], replicated, may hold values from 0.5 to 1.5
- norm_bias: float32 [1024], replicated, may hold values from -2.5 to 2.5
- w_query: bfloat16 [1024, 1024], P(None, 'heads'), may hold values from -0.375 to 0.375
- w_key: bfloat16 [1024, 1024], P(None, 'heads'), may hold values from -3.225 to 3.225
- w_value: bfloat16 [1024, 1024], P(None, 'heads'), may hold values from -0.1875 to 0.1875
- w_out: bfloat16 [1024, 1024], P('heads'), may hold values from -0.1875 to 0.1875
- layer_scale: float32 [1024], P('heads'), may hold values from 0.3 to 3
Outputs:
- layer_out: bfloat16 [16384, 1024], P('frames', 'heads')
The draws below stay inside these ranges and needn't reach their ends.
All inputs are finite; a program needn't handle non-finite values.
Results may differ from the reference program's by a relative error of at most 0.0092.
Values may be sent and summed in bfloat16 or wider, within the bound.
No kernel may reach another device: no remote copies, remote signals or barrier semaphores. Data moves between devices by JAX's collectives and lax.ppermute only.
A program may use at most 64 MiB of HBM per device.

```python
import math
import jax
import jax.numpy as jnp
from jax import lax

D = 1024
HEADS = 16
HEAD_DIM = 64
TOK_DEV = 512
TOKENS = 16384


def shared_base(key):
    return jnp.clip(jax.random.normal(key, (D, D), jnp.float32), -6.0, 6.0)


def draw_w_query(key, part):
    base = shared_base(key)
    return (base * (2.0 / math.sqrt(D))).astype(jnp.bfloat16)


def draw_w_key(key, part):
    key = jax.random.fold_in(key, 12)
    fresh = jnp.clip(jax.random.normal(key, (D, D), jnp.float32), -6.0, 6.0)
    return (fresh * (2.0 / math.sqrt(D))).astype(jnp.bfloat16)


def draw_tokens(key, part):
    key = jax.random.fold_in(key, 13)
    return jnp.clip(jax.random.normal(key, (TOKENS, D), jnp.float32), -5.0, 5.0).astype(jnp.bfloat16)


def shard_levels(key, dims, pieces, smallest, high):
    def one(axis_at, parts):
        draws = jax.random.uniform(jax.random.fold_in(jax.random.fold_in(key, 6), axis_at), (parts,), jnp.float32, smallest / len(pieces), high / len(pieces))
        return jnp.repeat(jnp.exp(draws), dims[axis_at] // parts).reshape((-1,) + (1,) * (len(dims) - axis_at - 1))

    gain = one(*pieces[0])
    for cut in pieces[1:]:
        gain = gain * one(*cut)
    return gain


def scatter_about(key, shape, width, most, cuts=(), held_as=jnp.bfloat16):
    result = jax.random.normal(key, shape, jnp.float32) * width
    if len(cuts) > 0:
        result = shard_levels(key, shape, cuts, -0.22, 0.18) * result
    return jnp.clip(result, min=-most, max=most).astype(held_as)


def setup_inputs(seed: int = 0) -> dict:
    splits = jax.random.split(jax.random.key(seed), 9)
    return {
        "tokens": draw_tokens(jax.random.fold_in(splits[8], 71), 0),
        "norm_gain": jnp.clip(1.0 + 0.1 * jax.random.normal(splits[1], (D,), jnp.float32), 0.5, 1.5),
        "norm_bias": scatter_about(splits[2], (D,), 0.5, 2.5, (), jnp.float32),
        "w_query": draw_w_query(jax.random.fold_in(splits[8], 71), 0),
        "w_key": draw_w_key(jax.random.fold_in(splits[8], 71), 0),
        "w_value": scatter_about(splits[5], (D, D), D ** -0.5, 0.1875, ((1, 8),)),
        "w_out": scatter_about(splits[6], (D, D), D ** -0.5, 0.1875, ((0, 8),)),
        "layer_scale": jnp.clip(jnp.exp(math.log(3.0) - 2.3025851 * jax.random.uniform(splits[7], (D,), jnp.float32) ** shard_levels(splits[7], (D,), ((0, 8),), -0.2, 0.2)), 0.3, 3.0),
    }


def normalize(values, norm_gain, norm_bias):
    centred = values - lax.optimization_barrier(jnp.mean(values, axis=-1, keepdims=True))
    variance = lax.optimization_barrier(jnp.mean(centred * centred, axis=-1, keepdims=True))
    return (centred * lax.rsqrt(variance + 1e-06) * norm_gain + norm_bias).astype(jnp.bfloat16)

def reference(tokens, norm_gain, norm_bias, w_query, w_key, w_value, w_out, layer_scale):
    normed = normalize(tokens.astype(jnp.float32), norm_gain, norm_bias)
    queries = jnp.dot(normed, w_query, preferred_element_type=jnp.float32).astype(jnp.bfloat16)
    keys = jnp.dot(normed, w_key, preferred_element_type=jnp.float32).astype(jnp.bfloat16)
    values = jnp.dot(normed, w_value, preferred_element_type=jnp.float32).astype(jnp.bfloat16)
    blocks = TOKENS // TOK_DEV
    scale_factor = HEAD_DIM ** (-0.5)

    def one_block(index):
        head = index // blocks
        block_index = index % blocks
        query_block = lax.dynamic_slice(queries, (block_index * TOK_DEV, head * HEAD_DIM), (TOK_DEV, HEAD_DIM))
        key_head = lax.dynamic_slice(keys, (jnp.int32(0), head * HEAD_DIM), (TOKENS, HEAD_DIM))
        value_head = lax.dynamic_slice(values, (jnp.int32(0), head * HEAD_DIM), (TOKENS, HEAD_DIM))
        scores = jnp.dot(query_block, key_head.T, preferred_element_type=jnp.float32) * scale_factor
        top = lax.optimization_barrier(jnp.max(scores, axis=-1, keepdims=True))
        weights = jnp.exp(scores - top)
        total = lax.optimization_barrier(jnp.sum(weights, axis=-1, keepdims=True))
        mixed = jnp.dot(weights.astype(jnp.bfloat16), value_head, preferred_element_type=jnp.float32)
        return (mixed / total).astype(jnp.bfloat16)
    indices = jnp.arange(HEADS * blocks, dtype=jnp.int32)
    results = lax.map(one_block, indices)
    attended = results.reshape(HEADS, blocks, TOK_DEV, HEAD_DIM).transpose(1, 2, 0, 3).reshape(TOKENS, D)
    projected = jnp.dot(attended, w_out, preferred_element_type=jnp.float32)
    return (tokens.astype(jnp.float32) + layer_scale * projected).astype(jnp.bfloat16)
```

```python
import functools

import jax
import jax.numpy as jnp
from jax import lax
from jax.experimental import pallas as pl
from jax.experimental.pallas import tpu as pltpu
from jax.sharding import PartitionSpec as P

HEAD_DIM = 64
HALF = 512
FEATURES = 1024
LOG2E = 1.4426950408889634
SCORE_SCALE = HEAD_DIM ** (-0.5) * LOG2E
PACK_ROWS = 80

Y_HI, Z, CORE = 2, 8, 2


def frames_shift(dy, dz, dc):
    pairs = []
    for y in range(Y_HI):
        for z in range(Z):
            for c in range(CORE):
                source = (y * Z + z) * CORE + c
                target = ((y ^ dy) * Z + (z + dz) % Z) * CORE + (c ^ dc)
                pairs.append((source, target))
    return pairs


def send(array, dy, dz, dc):
    return lax.ppermute(array, "frames", frames_shift(dy, dz, dc))


def params(limit=48):
    return pltpu.CompilerParams(vmem_limit_bytes=limit * 2**20)


def whole(count):
    return [pl.BlockSpec(memory_space=pltpu.VMEM)] * count


def project_kernel(
    core_ref, x_ref, gain_ref, bias_ref, wq_ref, wk_ref, wv_ref,
    q_keep, kv_keep, q_send, kv_send, normed_ref, all_ref,
):
    blocks = x_ref.shape[0]
    width = x_ref.shape[2]
    total = jnp.zeros((HALF, width), jnp.float32)
    for j in range(blocks):
        total = total + x_ref[j].astype(jnp.float32)
    mean = jnp.sum(total, axis=1, keepdims=True) * (1.0 / FEATURES)
    squares = jnp.zeros((HALF, width), jnp.float32)
    for j in range(blocks):
        centred = x_ref[j].astype(jnp.float32) - mean
        squares = squares + centred * centred
    variance = jnp.sum(squares, axis=1, keepdims=True) * (1.0 / FEATURES)
    inverse = lax.rsqrt(variance + 1e-06)
    for j in range(blocks):
        centred = x_ref[j].astype(jnp.float32) - mean
        normed = centred * inverse * gain_ref[j : j + 1, :] + bias_ref[j : j + 1, :]
        normed_ref[:, j * width : (j + 1) * width] = normed.astype(jnp.bfloat16)
    for k, w_ref in enumerate((wq_ref, wk_ref, wv_ref)):
        all_ref[k * 128 : (k + 1) * 128, :] = lax.dot_general(
            w_ref[...].T,
            normed_ref[...],
            (((1,), (1,)), ((), ())),
            preferred_element_type=jnp.float32,
        ).astype(jnp.bfloat16)
    core = core_ref[0]
    for q_out, kv_out, head in ((q_keep, kv_keep, core), (q_send, kv_send, 1 - core)):
        row = pl.multiple_of(head * HEAD_DIM, HEAD_DIM)
        q_out[...] = all_ref[pl.ds(row, HEAD_DIM), :]
        kv_out[0:HEAD_DIM, :] = all_ref[pl.ds(128 + row, HEAD_DIM), :]
        kv_out[HEAD_DIM : 2 * HEAD_DIM, :] = all_ref[pl.ds(256 + row, HEAD_DIM), :]


def project(core, x, gain, bias, wq, wk, wv):
    q_shape = jax.ShapeDtypeStruct((HEAD_DIM, HALF), jnp.bfloat16)
    kv_shape = jax.ShapeDtypeStruct((2 * HEAD_DIM, HALF), jnp.bfloat16)
    return pl.pallas_call(
        project_kernel,
        out_shape=(q_shape, kv_shape, q_shape, kv_shape),
        in_specs=[pl.BlockSpec(memory_space=pltpu.SMEM)] + whole(6),
        out_specs=tuple(whole(4)),
        scratch_shapes=[
            pltpu.VMEM((HALF, FEATURES), jnp.bfloat16),
            pltpu.VMEM((3 * 128, HALF), jnp.bfloat16),
        ],
        compiler_params=params(),
        name="norm_project",
        cost_estimate=pl.CostEstimate(
            flops=2 * HALF * FEATURES * 384, bytes_accessed=2 * 2**20, transcendentals=HALF
        ),
    )(core, x, gain, bias, wq, wk, wv)


def attend_kernel(*refs, tiles, work, fresh, pack):
    pairs = 1 + max(first + count - 1 for _, first, count in work)
    kv = refs[: 2 * pairs]
    at = 2 * pairs
    queries = refs[at : at + tiles]
    at += tiles
    old = None
    if not fresh:
        old = refs[at : at + 3 * tiles]
        at += 3 * tiles
    if pack:
        pack_ref = refs[at]
        at += 1
        new = None
    else:
        new = refs[at : at + 3 * tiles]
        at += 3 * tiles
    k_ref, vt_ref, s_ref = refs[at:]
    for b in range(2 * pairs):
        k_ref[b * HALF : (b + 1) * HALF, :] = kv[b][0:HEAD_DIM, :].T
        vt_ref[:, b * HALF : (b + 1) * HALF] = kv[b][HEAD_DIM:, :]

    block = 2 * HALF
    steps = []
    for tile, first, count in work:
        for p in range(first, first + count):
            steps.append((tile, p, p == first, p == first + count - 1))

    def score(tile, p, slot):
        s = jnp.dot(
            k_ref[p * block : (p + 1) * block, :],
            queries[tile][...],
            preferred_element_type=jnp.float32,
        )
        s_ref[slot] = s
        return jnp.max(s, axis=0, keepdims=True)

    top = score(steps[0][0], steps[0][1], 0)
    for n, (tile, p, first, last) in enumerate(steps):
        if first:
            if fresh:
                m = jnp.full((1, HALF), -jnp.inf, jnp.float32)
                l = jnp.zeros((1, HALF), jnp.float32)
                acc = jnp.zeros((HEAD_DIM, HALF), jnp.float32)
            else:
                m, l, acc = (old[3 * tile + i][...] for i in range(3))
        newest = jnp.maximum(m, top)
        factor = jnp.exp2((m - newest) * SCORE_SCALE)
        if n + 1 < len(steps):
            top = score(steps[n + 1][0], steps[n + 1][1], (n + 1) % 2)
        weights = jnp.exp2((s_ref[n % 2] - newest) * SCORE_SCALE)
        l = l * factor + jnp.sum(weights, axis=0, keepdims=True)
        acc = acc * factor + jnp.dot(
            vt_ref[:, p * block : (p + 1) * block],
            weights.astype(jnp.bfloat16),
            preferred_element_type=jnp.float32,
        )
        m = newest
        if last and not pack:
            new[3 * tile][...] = m
            new[3 * tile + 1][...] = l
            new[3 * tile + 2][...] = acc
        if last and pack:
            columns = slice(tile * HALF, (tile + 1) * HALF)
            pack_ref[0:HEAD_DIM, columns] = (acc / l).astype(jnp.bfloat16)
            lse = m * SCORE_SCALE + jnp.log2(l)
            high = lse.astype(jnp.bfloat16).astype(jnp.float32)
            middle = (lse - high).astype(jnp.bfloat16).astype(jnp.float32)
            low = lse - high - middle
            row = lax.broadcasted_iota(jnp.int32, (PACK_ROWS - HEAD_DIM, HALF), 0)
            rows = jnp.where(row == 0, high, jnp.where(row == 1, middle, low))
            pack_ref[HEAD_DIM:PACK_ROWS, columns] = rows.astype(jnp.bfloat16)


def attend(kv, queries, states, work, pack=False):
    tiles = len(queries)
    fresh = states is None
    state_shapes = (
        jax.ShapeDtypeStruct((1, HALF), jnp.float32),
        jax.ShapeDtypeStruct((1, HALF), jnp.float32),
        jax.ShapeDtypeStruct((HEAD_DIM, HALF), jnp.float32),
    ) * tiles
    if pack:
        out_shape = jax.ShapeDtypeStruct((PACK_ROWS, tiles * HALF), jnp.bfloat16)
        out_specs = whole(1)[0]
    else:
        out_shape = state_shapes
        out_specs = tuple(whole(3 * tiles))
    operands = list(kv) + list(queries) + ([] if fresh else list(states))
    count = sum(c for _, _, c in work)
    return pl.pallas_call(
        functools.partial(attend_kernel, tiles=tiles, work=work, fresh=fresh, pack=pack),
        out_shape=out_shape,
        in_specs=whole(len(operands)),
        out_specs=out_specs,
        scratch_shapes=[
            pltpu.VMEM((len(kv) * HALF, HEAD_DIM), jnp.bfloat16),
            pltpu.VMEM((HEAD_DIM, len(kv) * HALF), jnp.bfloat16),
            pltpu.VMEM((2, 2 * HALF, HALF), jnp.float32),
        ],
        compiler_params=params(),
        name="attend",
        cost_estimate=pl.CostEstimate(
            flops=count * 4 * HALF * 2 * HALF * HEAD_DIM * 4,
            bytes_accessed=2**20,
            transcendentals=count * 2 * HALF * HALF,
        ),
    )(*operands)


def combine_kernel(m0, l0, acc0, m1, l1, acc1, pack_ref, keep_ref, send_ref):
    for tile, (m, l, acc, out) in enumerate(
        ((m0, l0, acc0, keep_ref), (m1, l1, acc1, send_ref))
    ):
        columns = slice(tile * HALF, (tile + 1) * HALF)
        other = pack_ref[0:HEAD_DIM, columns].astype(jnp.float32)
        split = pack_ref[HEAD_DIM:PACK_ROWS, columns].astype(jnp.float32)
        other_lse = split[0:1] + split[1:2] + split[2:3]
        total = l[...]
        lse = m[...] * SCORE_SCALE + jnp.log2(total)
        top = jnp.maximum(lse, other_lse)
        mine = jnp.exp2(lse - top)
        theirs = jnp.exp2(other_lse - top)
        whole_weight = 1.0 / (mine + theirs)
        out[...] = (
            acc[...] * (mine * whole_weight / total) + other * (theirs * whole_weight)
        ).astype(jnp.bfloat16)


def combine(states, pack):
    shape = jax.ShapeDtypeStruct((HEAD_DIM, HALF), jnp.bfloat16)
    return pl.pallas_call(
        combine_kernel,
        out_shape=(shape, shape),
        in_specs=whole(7),
        out_specs=tuple(whole(2)),
        compiler_params=params(),
        name="combine",
    )(*states, pack)


def output_kernel(core_ref, mine_ref, theirs_ref, w_ref, out_ref):
    core = core_ref[0]
    mine_rows = pl.ds(pl.multiple_of(core * HEAD_DIM, HEAD_DIM), HEAD_DIM)
    their_rows = pl.ds(pl.multiple_of((1 - core) * HEAD_DIM, HEAD_DIM), HEAD_DIM)
    attended = jnp.concatenate([mine_ref[...], theirs_ref[...]], axis=0).T
    weights = jnp.concatenate([w_ref[mine_rows, :], w_ref[their_rows, :]], axis=0)
    width = out_ref.shape[2]
    for j in range(out_ref.shape[0]):
        out_ref[j] = jnp.dot(
            attended,
            weights[:, j * width : (j + 1) * width],
            preferred_element_type=jnp.float32,
        ).astype(jnp.bfloat16)


def output(core, mine, theirs, w_out, groups):
    return pl.pallas_call(
        output_kernel,
        out_shape=jax.ShapeDtypeStruct((groups, HALF, FEATURES // groups), jnp.bfloat16),
        in_specs=[pl.BlockSpec(memory_space=pltpu.SMEM)] + whole(3),
        out_specs=whole(1)[0],
        compiler_params=params(),
        name="output_project",
    )(core, mine, theirs, w_out)


def finish_kernel(parts_ref, tokens_ref, scale_ref, out_ref):
    total = parts_ref[0].astype(jnp.float32)
    for j in range(1, parts_ref.shape[0]):
        total = total + parts_ref[j].astype(jnp.float32)
    out_ref[...] = (tokens_ref[...].astype(jnp.float32) + scale_ref[...] * total).astype(
        jnp.bfloat16
    )


def finish(parts, tokens, layer_scale):
    return pl.pallas_call(
        finish_kernel,
        out_shape=jax.ShapeDtypeStruct(tokens.shape, jnp.bfloat16),
        in_specs=whole(3),
        out_specs=whole(1)[0],
        compiler_params=params(),
        name="finish",
    )(parts, tokens, layer_scale)


def per_device(tokens, norm_gain, norm_bias, w_query, w_key, w_value, w_out, layer_scale):
    groups = lax.axis_size("heads")
    width = FEATURES // groups
    core = (lax.axis_index("frames") % CORE).astype(jnp.int32).reshape(1)

    with jax.named_scope("gather_tokens"):
        spread = jnp.broadcast_to(tokens[None], (groups,) + tokens.shape)
        x = lax.all_to_all(spread, "heads", 0, 0, tiled=True)
    q_keep, kv_keep, q_send, kv_send = project(
        core,
        x,
        norm_gain.reshape(groups, width),
        norm_bias.reshape(groups, width),
        w_query,
        w_key,
        w_value,
    )

    right = [send(kv_keep, 0, 1, 0), send(kv_send, 0, 1, 1)]
    left = [send(kv_keep, 0, -1, 0), send(kv_send, 0, -1, 1)]
    own = [kv_keep, send(kv_send, 0, 0, 1)]
    queries = [q_keep, send(q_send, 0, 0, 1)]
    partner = [send(q_keep, 1, 0, 0), send(q_send, 1, 0, 1)]

    mine = attend(own, queries, None, ((0, 0, 1), (1, 0, 1)))
    theirs = None
    held = own
    for step in range(3):
        arrived = right + left
        if step < 2:
            right = [send(b, 0, 1, 0) for b in right]
            left = [send(b, 0, -1, 0) for b in left]
        else:
            last = [send(right[0], 0, 1, 0), send(left[1], 0, -1, 0)]
        if step == 0:
            theirs = attend(own + arrived, partner, None, ((0, 0, 3), (1, 0, 3)))
            mine = attend(arrived, queries, mine, ((0, 0, 2), (1, 0, 2)))
        else:
            both = attend(
                arrived,
                queries + partner,
                mine + theirs,
                ((0, 0, 2), (1, 0, 2), (2, 0, 2), (3, 0, 2)),
            )
            mine, theirs = both[:6], both[6:]
    packed = attend(last, partner, theirs, ((0, 0, 1), (1, 0, 1)), pack=True)
    received = send(packed, 1, 0, 0)
    mine = attend(last, queries, mine, ((0, 0, 1), (1, 0, 1)))
    att_keep, att_send = combine(mine, received)
    att_other = send(att_send, 0, 0, 1)
    partial_sums = output(core, att_keep, att_other, w_out, groups)
    with jax.named_scope("sum_heads"):
        parts = lax.all_to_all(partial_sums, "heads", 0, 0, tiled=True)
    return finish(parts, tokens, layer_scale.reshape(1, width))


def solution(mesh):
    in_specs = (
        P("frames", "heads"),
        P(),
        P(),
        P(None, "heads"),
        P(None, "heads"),
        P(None, "heads"),
        P("heads", None),
        P("heads"),
    )
    out_specs = P("frames", "heads")
    return jax.shard_map(
        per_device, mesh=mesh, in_specs=in_specs, out_specs=out_specs, check_vma=False
    )
```

```python
import functools

import jax
import jax.numpy as jnp
from jax import lax
from jax.experimental import pallas as pl
from jax.experimental.pallas import tpu as pltpu
from jax.sharding import PartitionSpec as P

HEAD_DIM = 64
HALF = 512
BLOCK = 1024
TILE = 512
FEATURES = 1024
LOG2E = 1.4426950408889634
SCORE_SCALE = HEAD_DIM ** (-0.5) * LOG2E
PACK_ROWS = 80

Y_HI, Z, CORE = 2, 8, 2


def frames_shift(dy, dz, dc):
    pairs = []
    for y in range(Y_HI):
        for z in range(Z):
            for c in range(CORE):
                source = (y * Z + z) * CORE + c
                target = ((y ^ dy) * Z + (z + dz) % Z) * CORE + (c ^ dc)
                pairs.append((source, target))
    return pairs


def send(array, dy, dz, dc):
    return lax.ppermute(array, "frames", frames_shift(dy, dz, dc))


def params(limit=48):
    return pltpu.CompilerParams(vmem_limit_bytes=limit * 2**20)


def whole(count):
    return [pl.BlockSpec(memory_space=pltpu.VMEM)] * count


def spread_kernel(tokens_ref, out_ref):
    for j in range(out_ref.shape[0]):
        out_ref[j] = tokens_ref[...]


def spread(tokens, groups):
    return pl.pallas_call(
        spread_kernel,
        out_shape=jax.ShapeDtypeStruct((groups,) + tokens.shape, tokens.dtype),
        in_specs=whole(1),
        out_specs=whole(1)[0],
        compiler_params=params(),
        name="spread",
    )(tokens)


def project_kernel(
    core_ref, x_ref, gain_ref, bias_ref, wq_ref, wk_ref, wv_ref, keep, give, normed_ref, all_ref
):
    blocks = x_ref.shape[0]
    width = x_ref.shape[2]
    total = jnp.zeros((HALF, width), jnp.float32)
    for j in range(blocks):
        total = total + x_ref[j].astype(jnp.float32)
    mean = jnp.sum(total, axis=1, keepdims=True) * (1.0 / FEATURES)
    squares = jnp.zeros((HALF, width), jnp.float32)
    for j in range(blocks):
        centred = x_ref[j].astype(jnp.float32) - mean
        squares = squares + centred * centred
    variance = jnp.sum(squares, axis=1, keepdims=True) * (1.0 / FEATURES)
    inverse = lax.rsqrt(variance + 1e-06)
    for j in range(blocks):
        centred = x_ref[j].astype(jnp.float32) - mean
        normed = centred * inverse * gain_ref[j : j + 1, :] + bias_ref[j : j + 1, :]
        normed_ref[:, j * width : (j + 1) * width] = normed.astype(jnp.bfloat16)
    for k, w_ref in enumerate((wq_ref, wk_ref, wv_ref)):
        all_ref[k * 128 : (k + 1) * 128, :] = lax.dot_general(
            w_ref[...].T,
            normed_ref[...],
            (((1,), (1,)), ((), ())),
            preferred_element_type=jnp.float32,
        ).astype(jnp.bfloat16)
    core = core_ref[0]
    for out, head in ((keep, core), (give, 1 - core)):
        row = pl.multiple_of(head * HEAD_DIM, HEAD_DIM)
        for k in range(3):
            out[k * HEAD_DIM : (k + 1) * HEAD_DIM, :] = all_ref[pl.ds(k * 128 + row, HEAD_DIM), :]


def project(core, x, gain, bias, wq, wk, wv):
    shape = jax.ShapeDtypeStruct((3 * HEAD_DIM, HALF), jnp.bfloat16)
    return pl.pallas_call(
        project_kernel,
        out_shape=(shape, shape),
        in_specs=[pl.BlockSpec(memory_space=pltpu.SMEM)] + whole(6),
        out_specs=tuple(whole(2)),
        scratch_shapes=[
            pltpu.VMEM((HALF, FEATURES), jnp.bfloat16),
            pltpu.VMEM((3 * 128, HALF), jnp.bfloat16),
        ],
        compiler_params=params(),
        name="norm_project",
        cost_estimate=pl.CostEstimate(
            flops=2 * HALF * FEATURES * 384, bytes_accessed=2 * 2**20, transcendentals=HALF
        ),
    )(core, x, gain, bias, wq, wk, wv)


def join_kernel(keep, taken, q_ref, kv_ref):
    for ref, columns in ((keep, slice(0, HALF)), (taken, slice(HALF, 2 * HALF))):
        q_ref[:, columns] = ref[0:HEAD_DIM, :]
        kv_ref[:, columns] = ref[HEAD_DIM:, :]


def join(keep, taken):
    return pl.pallas_call(
        join_kernel,
        out_shape=(
            jax.ShapeDtypeStruct((HEAD_DIM, 2 * HALF), jnp.bfloat16),
            jax.ShapeDtypeStruct((2 * HEAD_DIM, 2 * HALF), jnp.bfloat16),
        ),
        in_specs=whole(2),
        out_specs=tuple(whole(2)),
        compiler_params=params(),
        name="join",
    )(keep, taken)


def attend_kernel(*refs, blocks, sets, work, fresh, pack):
    kv = refs[:blocks]
    queries = refs[blocks : blocks + sets]
    at = blocks + sets
    old = None
    if not fresh:
        old = refs[at : at + 3 * sets]
        at += 3 * sets
    if pack:
        pack_ref = refs[at]
        at += 1
    else:
        new = refs[at : at + 3 * sets]
        at += 3 * sets
    k_ref, s_ref = refs[at:]
    for b in range(blocks):
        k_ref[b * BLOCK : (b + 1) * BLOCK, :] = kv[b][0:HEAD_DIM, :].T

    steps = []
    for which, chosen in work:
        for tile in range(BLOCK // TILE):
            for n, b in enumerate(chosen):
                steps.append((which, tile, b, n == 0, n == len(chosen) - 1))

    def score(which, tile, b, slot):
        s = jnp.dot(
            k_ref[b * BLOCK : (b + 1) * BLOCK, :],
            queries[which][:, tile * TILE : (tile + 1) * TILE],
            preferred_element_type=jnp.float32,
        )
        s_ref[slot] = s
        return jnp.max(s, axis=0, keepdims=True)

    top = score(*steps[0][:3], 0)
    for n, (which, tile, b, first, last) in enumerate(steps):
        columns = slice(tile * TILE, (tile + 1) * TILE)
        if first:
            if fresh:
                m = jnp.full((1, TILE), -jnp.inf, jnp.float32)
                l = jnp.zeros((1, TILE), jnp.float32)
                acc = jnp.zeros((HEAD_DIM, TILE), jnp.float32)
            else:
                m, l, acc = (old[3 * which + i][:, columns] for i in range(3))
        newest = jnp.maximum(m, top)
        factor = jnp.exp2((m - newest) * SCORE_SCALE)
        if n + 1 < len(steps):
            top = score(*steps[n + 1][:3], (n + 1) % 2)
        weights = jnp.exp2((s_ref[n % 2] - newest) * SCORE_SCALE)
        l = l * factor + jnp.sum(weights, axis=0, keepdims=True)
        acc = acc * factor + jnp.dot(
            kv[b][HEAD_DIM:, :],
            weights.astype(jnp.bfloat16),
            preferred_element_type=jnp.float32,
        )
        m = newest
        if last and not pack:
            new[3 * which][:, columns] = m
            new[3 * which + 1][:, columns] = l
            new[3 * which + 2][:, columns] = acc
        if last and pack:
            pack_ref[0:HEAD_DIM, columns] = (acc / l).astype(jnp.bfloat16)
            lse = m * SCORE_SCALE + jnp.log2(l)
            high = lse.astype(jnp.bfloat16).astype(jnp.float32)
            middle = (lse - high).astype(jnp.bfloat16).astype(jnp.float32)
            low = lse - high - middle
            row = lax.broadcasted_iota(jnp.int32, (PACK_ROWS - HEAD_DIM, TILE), 0)
            rows = jnp.where(row == 0, high, jnp.where(row == 1, middle, low))
            pack_ref[HEAD_DIM:PACK_ROWS, columns] = rows.astype(jnp.bfloat16)


def attend(kv, queries, states, work, pack=False):
    sets = len(queries)
    fresh = states is None
    state_shapes = (
        jax.ShapeDtypeStruct((1, BLOCK), jnp.float32),
        jax.ShapeDtypeStruct((1, BLOCK), jnp.float32),
        jax.ShapeDtypeStruct((HEAD_DIM, BLOCK), jnp.float32),
    ) * sets
    if pack:
        out_shape = jax.ShapeDtypeStruct((PACK_ROWS, BLOCK), jnp.bfloat16)
        out_specs = whole(1)[0]
    else:
        out_shape = state_shapes
        out_specs = tuple(whole(3 * sets))
    operands = list(kv) + list(queries) + ([] if fresh else list(states))
    count = sum(len(chosen) for _, chosen in work)
    return pl.pallas_call(
        functools.partial(
            attend_kernel, blocks=len(kv), sets=sets, work=work, fresh=fresh, pack=pack
        ),
        out_shape=out_shape,
        in_specs=whole(len(operands)),
        out_specs=out_specs,
        scratch_shapes=[
            pltpu.VMEM((len(kv) * BLOCK, HEAD_DIM), jnp.bfloat16),
            pltpu.VMEM((2, BLOCK, TILE), jnp.float32),
        ],
        compiler_params=params(),
        name="attend",
        cost_estimate=pl.CostEstimate(
            flops=count * 4 * BLOCK * BLOCK * HEAD_DIM * 4,
            bytes_accessed=2**20,
            transcendentals=count * BLOCK * BLOCK,
        ),
    )(*operands)


def combine_kernel(m, l, acc, pack_ref, keep_ref, give_ref):
    for tile, out in enumerate((keep_ref, give_ref)):
        columns = slice(tile * HALF, (tile + 1) * HALF)
        other = pack_ref[0:HEAD_DIM, columns].astype(jnp.float32)
        split = pack_ref[HEAD_DIM:PACK_ROWS, columns].astype(jnp.float32)
        other_lse = split[0:1] + split[1:2] + split[2:3]
        total = l[:, columns]
        lse = m[:, columns] * SCORE_SCALE + jnp.log2(total)
        top = jnp.maximum(lse, other_lse)
        mine = jnp.exp2(lse - top)
        theirs = jnp.exp2(other_lse - top)
        inverse = 1.0 / (mine + theirs)
        out[...] = (
            acc[:, columns] * (mine * inverse / total) + other * (theirs * inverse)
        ).astype(jnp.bfloat16)


def combine(states, pack):
    shape = jax.ShapeDtypeStruct((HEAD_DIM, HALF), jnp.bfloat16)
    return pl.pallas_call(
        combine_kernel,
        out_shape=(shape, shape),
        in_specs=whole(4),
        out_specs=tuple(whole(2)),
        compiler_params=params(),
        name="combine",
    )(*states, pack)


def output_kernel(core_ref, mine_ref, theirs_ref, w_ref, out_ref):
    core = core_ref[0]
    mine_rows = pl.ds(pl.multiple_of(core * HEAD_DIM, HEAD_DIM), HEAD_DIM)
    their_rows = pl.ds(pl.multiple_of((1 - core) * HEAD_DIM, HEAD_DIM), HEAD_DIM)
    attended = jnp.concatenate([mine_ref[...], theirs_ref[...]], axis=0).T
    weights = jnp.concatenate([w_ref[mine_rows, :], w_ref[their_rows, :]], axis=0)
    width = out_ref.shape[2]
    for j in range(out_ref.shape[0]):
        out_ref[j] = jnp.dot(
            attended,
            weights[:, j * width : (j + 1) * width],
            preferred_element_type=jnp.float32,
        ).astype(jnp.bfloat16)


def output(core, mine, theirs, w_out, groups):
    return pl.pallas_call(
        output_kernel,
        out_shape=jax.ShapeDtypeStruct((groups, HALF, FEATURES // groups), jnp.bfloat16),
        in_specs=[pl.BlockSpec(memory_space=pltpu.SMEM)] + whole(3),
        out_specs=whole(1)[0],
        compiler_params=params(),
        name="output_project",
    )(core, mine, theirs, w_out)


def finish_kernel(parts_ref, tokens_ref, scale_ref, out_ref):
    total = parts_ref[0].astype(jnp.float32)
    for j in range(1, parts_ref.shape[0]):
        total = total + parts_ref[j].astype(jnp.float32)
    out_ref[...] = (tokens_ref[...].astype(jnp.float32) + scale_ref[...] * total).astype(
        jnp.bfloat16
    )


def finish(parts, tokens, layer_scale):
    return pl.pallas_call(
        finish_kernel,
        out_shape=jax.ShapeDtypeStruct(tokens.shape, jnp.bfloat16),
        in_specs=whole(3),
        out_specs=whole(1)[0],
        compiler_params=params(),
        name="finish",
    )(parts, tokens, layer_scale)


def per_device(tokens, norm_gain, norm_bias, w_query, w_key, w_value, w_out, layer_scale):
    groups = lax.axis_size("heads")
    width = FEATURES // groups
    core = (lax.axis_index("frames") % CORE).astype(jnp.int32).reshape(1)

    x = lax.all_to_all(spread(tokens, groups), "heads", 0, 0, tiled=True)
    keep, give = project(
        core,
        x,
        norm_gain.reshape(groups, width),
        norm_bias.reshape(groups, width),
        w_query,
        w_key,
        w_value,
    )
    queries, own = join(keep, send(give, 0, 0, 1))
    right, left = own, own
    mine, theirs = None, None
    for step in range(4):
        near = (right, left)
        right = send(right, 0, 1, 0)
        if step < 3:
            left = send(left, 0, -1, 0)
        if step == 0:
            partner = send(queries, 1, 0, 0)
            mine = attend([own], [queries], None, ((0, (0,)),))
        elif step == 1:
            late = near[1]
            theirs = attend([own, *near], [partner], None, ((0, (0, 1, 2)),))
            mine = attend(near[:1], [queries], mine, ((0, (0,)),))
        else:
            both = attend(
                near, [queries, partner], mine + theirs, ((0, (0, 1)), (1, (0, 1)))
            )
            mine, theirs = both[:3], both[3:]
    packed = attend([right], [partner], theirs, ((0, (0,)),), pack=True)
    received = send(packed, 1, 0, 0)
    mine = attend([late, right], [queries], mine, ((0, (0, 1)),))
    att_keep, att_send = combine(mine, received)
    att_other = send(att_send, 0, 0, 1)
    partial_sums = output(core, att_keep, att_other, w_out, groups)
    with jax.named_scope("sum_heads"):
        parts = lax.all_to_all(partial_sums, "heads", 0, 0, tiled=True)
    return finish(parts, tokens, layer_scale.reshape(1, width))


def solution(mesh):
    in_specs = (
        P("frames", "heads"),
        P(),
        P(),
        P(None, "heads"),
        P(None, "heads"),
        P(None, "heads"),
        P("heads", None),
        P("heads"),
    )
    out_specs = P("frames", "heads")
    return jax.shard_map(
        per_device, mesh=mesh, in_specs=in_specs, out_specs=out_specs, check_vma=False
    )
```

```python
import functools

import jax
import jax.numpy as jnp
from jax import lax
from jax.experimental import pallas as pl
from jax.experimental.pallas import tpu as pltpu
from jax.sharding import PartitionSpec as P

HEAD_DIM = 64
HALF = 512
BLOCK = 1024
TILE = 512
FEATURES = 1024
LOG2E = 1.4426950408889634
SCORE_SCALE = HEAD_DIM ** (-0.5) * LOG2E
PACK_ROWS = 80

Y_HI, Z, CORE = 2, 8, 2


def frames_shift(dy, dz, dc):
    pairs = []
    for y in range(Y_HI):
        for z in range(Z):
            for c in range(CORE):
                source = (y * Z + z) * CORE + c
                target = ((y ^ dy) * Z + (z + dz) % Z) * CORE + (c ^ dc)
                pairs.append((source, target))
    return pairs


def send(array, dy, dz, dc):
    return lax.ppermute(array, "frames", frames_shift(dy, dz, dc))


X, Y_LO = 4, 2
STEPS = ((0, 0), (0, 1), (1, 0), (3, 0), (2, 0), (1, 1), (3, 1), (2, 1))


def heads_shift(dx, dy):
    return [
        (x * Y_LO + y, ((x + dx) % X) * Y_LO + (y ^ dy)) for x in range(X) for y in range(Y_LO)
    ]


def send_heads(array, step):
    return lax.ppermute(array, "heads", heads_shift(*step))


def params(limit=48):
    return pltpu.CompilerParams(vmem_limit_bytes=limit * 2**20)


def whole(count):
    return [pl.BlockSpec(memory_space=pltpu.VMEM)] * count


def prepare_kernel(
    place_ref, wq_ref, wk_ref, wv_ref, w_out_ref, gain_ref, bias_ref, scale_ref,
    w_ref, out_ref, vectors_ref, flipped_ref,
):
    core = place_ref[0]
    heads = [pl.ds(pl.multiple_of(h * HEAD_DIM, HEAD_DIM), HEAD_DIM) for h in (core, 1 - core)]
    count = len(STEPS)
    width = FEATURES // count

    def columns(n):
        return pl.ds(pl.multiple_of(place_ref[n] * width, width), width)

    for k, ref in enumerate((wq_ref, wk_ref, wv_ref)):
        flipped_ref[...] = ref[...].T
        for h, rows in enumerate(heads):
            at = (3 * h + k) * HEAD_DIM
            for n in range(count):
                w_ref[at : at + HEAD_DIM, n * width : (n + 1) * width] = flipped_ref[
                    rows, columns(1 + n)
                ]
    for h, rows in enumerate(heads):
        for n in range(count):
            out_ref[h * HEAD_DIM : (h + 1) * HEAD_DIM, n * width : (n + 1) * width] = w_out_ref[
                rows, columns(1 + count + n)
            ]
    for n in range(count):
        j = place_ref[1 + n]
        vectors_ref[n : n + 1, :] = gain_ref[pl.ds(j, 1), :]
        vectors_ref[count + n : count + n + 1, :] = bias_ref[pl.ds(j, 1), :]
    vectors_ref[2 * count : 3 * count, :] = jnp.broadcast_to(scale_ref[...], (count, width))


def prepare(place, wq, wk, wv, w_out, gain, bias, scale):
    return pl.pallas_call(
        prepare_kernel,
        out_shape=(
            jax.ShapeDtypeStruct((6 * HEAD_DIM, FEATURES), jnp.bfloat16),
            jax.ShapeDtypeStruct((2 * HEAD_DIM, FEATURES), jnp.bfloat16),
            jax.ShapeDtypeStruct((3 * len(STEPS), FEATURES // len(STEPS)), jnp.float32),
        ),
        in_specs=[pl.BlockSpec(memory_space=pltpu.SMEM)] + whole(7),
        out_specs=tuple(whole(3)),
        scratch_shapes=[pltpu.VMEM((2 * HEAD_DIM, FEATURES), jnp.bfloat16)],
        compiler_params=params(),
        name="prepare",
        cost_estimate=pl.CostEstimate(
            flops=2 * HALF * FEATURES * 384, bytes_accessed=4 * 2**20, transcendentals=0
        ),
    )(place, wq, wk, wv, w_out, gain, bias, scale)


def project_kernel(*refs):
    x_refs = refs[:8]
    vectors_ref, w_ref, keep, give, normed_ref = refs[8:]
    count = len(x_refs)
    width = x_refs[0].shape[1]
    total = jnp.zeros((HALF, width), jnp.float32)
    for x_ref in x_refs:
        total = total + x_ref[...].astype(jnp.float32)
    mean = jnp.sum(total, axis=1, keepdims=True) * (1.0 / FEATURES)
    squares = jnp.zeros((HALF, width), jnp.float32)
    for x_ref in x_refs:
        centred = x_ref[...].astype(jnp.float32) - mean
        squares = squares + centred * centred
    variance = jnp.sum(squares, axis=1, keepdims=True) * (1.0 / FEATURES)
    inverse = lax.rsqrt(variance + 1e-06)
    for n, x_ref in enumerate(x_refs):
        centred = x_ref[...].astype(jnp.float32) - mean
        gain = vectors_ref[n : n + 1, :]
        bias = vectors_ref[count + n : count + n + 1, :]
        normed = centred * inverse * gain + bias
        normed_ref[:, n * width : (n + 1) * width] = normed.astype(jnp.bfloat16)
    for h, out in enumerate((keep, give)):
        out[...] = lax.dot_general(
            w_ref[h * 3 * HEAD_DIM : (h + 1) * 3 * HEAD_DIM, :],
            normed_ref[...],
            (((1,), (1,)), ((), ())),
            preferred_element_type=jnp.float32,
        ).astype(jnp.bfloat16)


def project(blocks, vectors, w):
    shape = jax.ShapeDtypeStruct((3 * HEAD_DIM, HALF), jnp.bfloat16)
    return pl.pallas_call(
        project_kernel,
        out_shape=(shape, shape),
        in_specs=whole(10),
        out_specs=tuple(whole(2)),
        scratch_shapes=[pltpu.VMEM((HALF, FEATURES), jnp.bfloat16)],
        compiler_params=params(),
        name="norm_project",
        cost_estimate=pl.CostEstimate(
            flops=2 * HALF * FEATURES * 384, bytes_accessed=2 * 2**20, transcendentals=HALF
        ),
    )(*blocks, vectors, w)


def join_kernel(keep, taken, q_ref, kv_ref):
    for ref, columns in ((keep, slice(0, HALF)), (taken, slice(HALF, 2 * HALF))):
        q_ref[:, columns] = ref[0:HEAD_DIM, :]
        kv_ref[:, columns] = ref[HEAD_DIM:, :]


def join(keep, taken):
    return pl.pallas_call(
        join_kernel,
        out_shape=(
            jax.ShapeDtypeStruct((HEAD_DIM, 2 * HALF), jnp.bfloat16),
            jax.ShapeDtypeStruct((2 * HEAD_DIM, 2 * HALF), jnp.bfloat16),
        ),
        in_specs=whole(2),
        out_specs=tuple(whole(2)),
        compiler_params=params(),
        name="join",
    )(keep, taken)


def attend_kernel(*refs, blocks, sets, work, fresh, pack):
    kv = refs[:blocks]
    queries = refs[blocks : blocks + sets]
    at = blocks + sets
    old = None
    if not fresh:
        old = refs[at : at + 3 * sets]
        at += 3 * sets
    new = None
    packs = refs[at : at + len(pack)]
    at += len(pack)
    if len(pack) < BLOCK // TILE:
        new = refs[at : at + 3 * sets]
        at += 3 * sets
    k_ref, s_ref = refs[at:]
    for b in range(blocks):
        k_ref[b * BLOCK : (b + 1) * BLOCK, :] = kv[b][0:HEAD_DIM, :].T

    steps = []
    for which, chosen in work:
        for tile in range(BLOCK // TILE):
            for n, b in enumerate(chosen):
                steps.append((which, tile, b, n == 0, n == len(chosen) - 1))

    def score(which, tile, b, slot):
        s = jnp.dot(
            k_ref[b * BLOCK : (b + 1) * BLOCK, :],
            queries[which][:, tile * TILE : (tile + 1) * TILE],
            preferred_element_type=jnp.float32,
        )
        s_ref[slot] = s
        return jnp.max(s, axis=0, keepdims=True)

    top = score(*steps[0][:3], 0)
    for n, (which, tile, b, first, last) in enumerate(steps):
        columns = slice(tile * TILE, (tile + 1) * TILE)
        if first:
            if fresh:
                m = jnp.full((1, TILE), -jnp.inf, jnp.float32)
                l = jnp.zeros((1, TILE), jnp.float32)
                acc = jnp.zeros((HEAD_DIM, TILE), jnp.float32)
            else:
                m, l, acc = (old[3 * which + i][:, columns] for i in range(3))
        newest = jnp.maximum(m, top)
        factor = jnp.exp2((m - newest) * SCORE_SCALE)
        if n + 1 < len(steps):
            top = score(*steps[n + 1][:3], (n + 1) % 2)
        weights = jnp.exp2((s_ref[n % 2] - newest) * SCORE_SCALE)
        l = l * factor + jnp.sum(weights, axis=0, keepdims=True)
        acc = acc * factor + jnp.dot(
            kv[b][HEAD_DIM:, :],
            weights.astype(jnp.bfloat16),
            preferred_element_type=jnp.float32,
        )
        m = newest
        if last and tile not in pack:
            new[3 * which][:, columns] = m
            new[3 * which + 1][:, columns] = l
            new[3 * which + 2][:, columns] = acc
        if last and tile in pack:
            pack_ref = packs[pack.index(tile)]
            pack_ref[0:HEAD_DIM, :] = (acc / l).astype(jnp.bfloat16)
            lse = m * SCORE_SCALE + jnp.log2(l)
            high = lse.astype(jnp.bfloat16).astype(jnp.float32)
            middle = (lse - high).astype(jnp.bfloat16).astype(jnp.float32)
            low = lse - high - middle
            row = lax.broadcasted_iota(jnp.int32, (PACK_ROWS - HEAD_DIM, TILE), 0)
            rows = jnp.where(row == 0, high, jnp.where(row == 1, middle, low))
            pack_ref[HEAD_DIM:PACK_ROWS, :] = rows.astype(jnp.bfloat16)


def attend(kv, queries, states, work, pack=()):
    sets = len(queries)
    fresh = states is None
    width = BLOCK if not pack else TILE
    out_shape = [jax.ShapeDtypeStruct((PACK_ROWS, TILE), jnp.bfloat16)] * len(pack)
    if len(pack) < BLOCK // TILE:
        out_shape += [
            jax.ShapeDtypeStruct((1, width), jnp.float32),
            jax.ShapeDtypeStruct((1, width), jnp.float32),
            jax.ShapeDtypeStruct((HEAD_DIM, width), jnp.float32),
        ] * sets
    operands = list(kv) + list(queries) + ([] if fresh else list(states))
    count = sum(len(chosen) for _, chosen in work)
    return pl.pallas_call(
        functools.partial(
            attend_kernel, blocks=len(kv), sets=sets, work=work, fresh=fresh, pack=pack
        ),
        out_shape=tuple(out_shape),
        in_specs=whole(len(operands)),
        out_specs=tuple(whole(len(out_shape))),
        scratch_shapes=[
            pltpu.VMEM((len(kv) * BLOCK, HEAD_DIM), jnp.bfloat16),
            pltpu.VMEM((2, BLOCK, TILE), jnp.float32),
        ],
        compiler_params=params(),
        name="attend",
        cost_estimate=pl.CostEstimate(
            flops=count * 4 * BLOCK * BLOCK * HEAD_DIM * 4,
            bytes_accessed=2**20,
            transcendentals=count * BLOCK * BLOCK,
        ),
    )(*operands)


def unpack(pack_ref):
    split = pack_ref[HEAD_DIM:PACK_ROWS, :].astype(jnp.float32)
    return pack_ref[0:HEAD_DIM, :].astype(jnp.float32), split[0:1] + split[1:2] + split[2:3]


def merge(first, first_lse, second, second_lse):
    top = jnp.maximum(first_lse, second_lse)
    a = jnp.exp2(first_lse - top)
    b = jnp.exp2(second_lse - top)
    inverse = 1.0 / (a + b)
    return (first * (a * inverse) + second * (b * inverse)).astype(jnp.bfloat16)


def output_kernel(m_ref, l_ref, acc_ref, mine_ref, core_ref, diagonal_ref, w_ref, *out_refs):
    total = l_ref[...]
    here = merge(
        acc_ref[...] / total, m_ref[...] * SCORE_SCALE + jnp.log2(total), *unpack(mine_ref)
    )
    other = merge(*unpack(core_ref), *unpack(diagonal_ref))
    attended = jnp.concatenate([here, other], axis=0).T
    width = out_refs[0].shape[1]
    for n, out_ref in enumerate(out_refs):
        out_ref[...] = jnp.dot(
            attended,
            w_ref[:, n * width : (n + 1) * width],
            preferred_element_type=jnp.float32,
        ).astype(jnp.bfloat16)


def output(state, mine, core, diagonal, w_out):
    shape = jax.ShapeDtypeStruct((HALF, FEATURES // len(STEPS)), jnp.bfloat16)
    return pl.pallas_call(
        output_kernel,
        out_shape=(shape,) * len(STEPS),
        in_specs=whole(7),
        out_specs=tuple(whole(len(STEPS))),
        compiler_params=params(),
        name="output_project",
    )(*state, mine, core, diagonal, w_out)


def add_kernel(*refs):
    total = refs[0][...].astype(jnp.float32)
    for ref in refs[1:-1]:
        total = total + ref[...].astype(jnp.float32)
    refs[-1][...] = total.astype(jnp.bfloat16)


def add(*terms):
    return pl.pallas_call(
        add_kernel,
        out_shape=jax.ShapeDtypeStruct(terms[0].shape, jnp.bfloat16),
        in_specs=whole(len(terms)),
        out_specs=whole(1)[0],
        compiler_params=params(),
        name="add",
    )(*terms)


def finish_kernel(tokens_ref, vectors_ref, *refs):
    out_ref = refs[-1]
    total = refs[0][...].astype(jnp.float32)
    for part_ref in refs[1:-1]:
        total = total + part_ref[...].astype(jnp.float32)
    scale = vectors_ref[2 * len(STEPS) : 2 * len(STEPS) + 1, :]
    out_ref[...] = (tokens_ref[...].astype(jnp.float32) + scale * total).astype(jnp.bfloat16)


def finish(parts, tokens, vectors):
    return pl.pallas_call(
        finish_kernel,
        out_shape=jax.ShapeDtypeStruct(tokens.shape, jnp.bfloat16),
        in_specs=whole(2 + len(parts)),
        out_specs=whole(1)[0],
        compiler_params=params(),
        name="finish",
    )(tokens, vectors, *parts)


def per_device(tokens, norm_gain, norm_bias, w_query, w_key, w_value, w_out, layer_scale):
    groups = lax.axis_size("heads")
    width = FEATURES // groups
    core = lax.axis_index("frames") % CORE
    x, y = lax.axis_index("heads") // Y_LO, lax.axis_index("heads") % Y_LO
    sources = [((x - dx) % X) * Y_LO + (y ^ dy) for dx, dy in STEPS]
    targets = [((x + dx) % X) * Y_LO + (y ^ dy) for dx, dy in STEPS]
    place = jnp.stack([core, *sources, *targets]).astype(jnp.int32)

    across = send_heads(tokens, (2, 0))
    beside = send_heads(tokens, (0, 1))
    blocks = [tokens, beside, send_heads(tokens, (1, 0)), send_heads(tokens, (3, 0)), across]
    blocks += [send_heads(beside, (1, 0)), send_heads(beside, (3, 0)), send_heads(across, (0, 1))]
    w_all, w_last, vectors = prepare(
        place,
        w_query,
        w_key,
        w_value,
        w_out,
        norm_gain.reshape(groups, width),
        norm_bias.reshape(groups, width),
        layer_scale.reshape(1, width),
    )
    keep, give = project(blocks, vectors, w_all)
    queries, own = join(keep, send(give, 0, 0, 1))
    right, left = own, own
    mine, theirs = None, None
    for step in range(4):
        near = (right, left)
        right = send(right, 0, 1, 0)
        if step < 3:
            left = send(left, 0, -1, 0)
        if step == 0:
            partner = send(queries, 1, 0, 0)
            mine = attend([own], [queries], None, ((0, (0,)),))
        elif step == 1:
            late = near[1]
            theirs = attend([own, *near], [partner], None, ((0, (0, 1, 2)),))
            mine = attend(near[:1], [queries], mine, ((0, (0,)),))
        else:
            both = attend(
                near, [queries, partner], mine + theirs, ((0, (0, 1)), (1, (0, 1)))
            )
            mine, theirs = both[:3], both[3:]
    for_mine, for_other = attend([right], [partner], theirs, ((0, (0,)),), pack=(0, 1))
    from_partner = send(for_mine, 1, 0, 0)
    from_diagonal = send(for_other, 1, 0, 1)
    for_core, *state = attend([late, right], [queries], mine, ((0, (0, 1)),), pack=(1,))
    from_core = send(for_core, 0, 0, 1)
    terms = dict(zip(STEPS, output(state, from_partner, from_core, from_diagonal, w_last)))
    by_partner = send_heads(terms[2, 1], (0, 1))
    by_column = [send_heads(terms[1, 1], (1, 0)), send_heads(terms[3, 1], (3, 0))]
    parts = [send_heads(add(terms[2, 0], by_partner), (2, 0))]
    parts += [send_heads(add(terms[0, 1], *by_column), (0, 1))]
    parts += [send_heads(terms[1, 0], (1, 0)), send_heads(terms[3, 0], (3, 0)), terms[0, 0]]
    return finish(parts, tokens, vectors)


def solution(mesh):
    in_specs = (
        P("frames", "heads"),
        P(),
        P(),
        P(None, "heads"),
        P(None, "heads"),
        P(None, "heads"),
        P("heads", None),
        P("heads"),
    )
    out_specs = P("frames", "heads")
    return jax.shard_map(
        per_device, mesh=mesh, in_specs=in_specs, out_specs=out_specs, check_vma=False
    )
```

```python
import functools

import jax
import jax.numpy as jnp
from jax import lax
from jax.experimental import pallas as pl
from jax.experimental.pallas import tpu as pltpu
from jax.sharding import PartitionSpec as P

HEAD_DIM = 64
HALF = 512
BLOCK = 1024
TILE = 512
FEATURES = 1024
LOG2E = 1.4426950408889634
SCORE_SCALE = HEAD_DIM ** (-0.5) * LOG2E
PACK_ROWS = 80

Y_HI, Z, CORE = 2, 8, 2


def frames_shift(dy, dz, dc):
    pairs = []
    for y in range(Y_HI):
        for z in range(Z):
            for c in range(CORE):
                source = (y * Z + z) * CORE + c
                target = ((y ^ dy) * Z + (z + dz) % Z) * CORE + (c ^ dc)
                pairs.append((source, target))
    return pairs


def send(array, dy, dz, dc):
    return lax.ppermute(array, "frames", frames_shift(dy, dz, dc))


X, Y_LO = 4, 2
STEPS = ((0, 0), (0, 1), (1, 0), (3, 0), (2, 0), (1, 1), (3, 1), (2, 1))


def heads_shift(dx, dy):
    return [
        (x * Y_LO + y, ((x + dx) % X) * Y_LO + (y ^ dy)) for x in range(X) for y in range(Y_LO)
    ]


def send_heads(array, step):
    return lax.ppermute(array, "heads", heads_shift(*step))


def params(limit=48):
    return pltpu.CompilerParams(vmem_limit_bytes=limit * 2**20)


def whole(count):
    return [pl.BlockSpec(memory_space=pltpu.VMEM)] * count


def prepare_kernel(
    place_ref, wq_hbm, wk_hbm, wv_hbm, w_out_hbm, gain_hbm, bias_hbm, scale_hbm,
    w_ref, out_ref, vectors_ref,
    wq_ref, wk_ref, wv_ref, w_out_ref, gain_ref, bias_ref, scale_ref, flipped_ref, done,
):
    pairs = (
        (wq_hbm, wq_ref), (wk_hbm, wk_ref), (wv_hbm, wv_ref), (w_out_hbm, w_out_ref),
        (gain_hbm, gain_ref), (bias_hbm, bias_ref), (scale_hbm, scale_ref),
    )
    copies = [pltpu.make_async_copy(a, b, done.at[n]) for n, (a, b) in enumerate(pairs)]
    for copy in copies:
        copy.start()
    for copy in copies:
        copy.wait()
    core = place_ref[0]
    heads = [pl.ds(pl.multiple_of(h * HEAD_DIM, HEAD_DIM), HEAD_DIM) for h in (core, 1 - core)]
    count = len(STEPS)
    width = FEATURES // count

    def columns(n):
        return pl.ds(pl.multiple_of(place_ref[n] * width, width), width)

    for k, ref in enumerate((wq_ref, wk_ref, wv_ref)):
        flipped_ref[...] = ref[...].T
        for h, rows in enumerate(heads):
            at = (3 * h + k) * HEAD_DIM
            for n in range(count):
                w_ref[at : at + HEAD_DIM, n * width : (n + 1) * width] = flipped_ref[
                    rows, columns(1 + n)
                ]
    for h, rows in enumerate(heads):
        for n in range(count):
            out_ref[h * HEAD_DIM : (h + 1) * HEAD_DIM, n * width : (n + 1) * width] = w_out_ref[
                rows, columns(1 + count + n)
            ]
    for n in range(count):
        j = place_ref[1 + n]
        vectors_ref[n : n + 1, :] = gain_ref[pl.ds(j, 1), :]
        vectors_ref[count + n : count + n + 1, :] = bias_ref[pl.ds(j, 1), :]
    vectors_ref[2 * count : 3 * count, :] = jnp.broadcast_to(scale_ref[...], (count, width))


def prepare(place, wq, wk, wv, w_out, gain, bias, scale):
    return pl.pallas_call(
        prepare_kernel,
        out_shape=(
            jax.ShapeDtypeStruct((6 * HEAD_DIM, FEATURES), jnp.bfloat16),
            jax.ShapeDtypeStruct((2 * HEAD_DIM, FEATURES), jnp.bfloat16),
            jax.ShapeDtypeStruct((3 * len(STEPS), FEATURES // len(STEPS)), jnp.float32),
        ),
        in_specs=[pl.BlockSpec(memory_space=pltpu.SMEM)]
        + [pl.BlockSpec(memory_space=pltpu.MemorySpace.HBM)] * 7,
        out_specs=tuple(whole(3)),
        scratch_shapes=[
            pltpu.VMEM(a.shape, a.dtype) for a in (wq, wk, wv, w_out, gain, bias, scale)
        ]
        + [pltpu.VMEM((2 * HEAD_DIM, FEATURES), jnp.bfloat16), pltpu.SemaphoreType.DMA((7,))],
        compiler_params=params(),
        name="prepare",
        cost_estimate=pl.CostEstimate(
            flops=2 * HALF * FEATURES * 384, bytes_accessed=4 * 2**20, transcendentals=0
        ),
    )(place, wq, wk, wv, w_out, gain, bias, scale)


def project_kernel(*refs):
    x_refs = refs[:8]
    vectors_ref, w_ref, keep, give, normed_ref = refs[8:]
    count = len(x_refs)
    width = x_refs[0].shape[1]
    total = jnp.zeros((HALF, width), jnp.float32)
    for x_ref in x_refs:
        total = total + x_ref[...].astype(jnp.float32)
    mean = jnp.sum(total, axis=1, keepdims=True) * (1.0 / FEATURES)
    squares = jnp.zeros((HALF, width), jnp.float32)
    for x_ref in x_refs:
        centred = x_ref[...].astype(jnp.float32) - mean
        squares = squares + centred * centred
    variance = jnp.sum(squares, axis=1, keepdims=True) * (1.0 / FEATURES)
    inverse = lax.rsqrt(variance + 1e-06)
    for n, x_ref in enumerate(x_refs):
        centred = x_ref[...].astype(jnp.float32) - mean
        gain = vectors_ref[n : n + 1, :]
        bias = vectors_ref[count + n : count + n + 1, :]
        normed = centred * inverse * gain + bias
        normed_ref[:, n * width : (n + 1) * width] = normed.astype(jnp.bfloat16)
    for h, out in enumerate((keep, give)):
        out[...] = lax.dot_general(
            w_ref[h * 3 * HEAD_DIM : (h + 1) * 3 * HEAD_DIM, :],
            normed_ref[...],
            (((1,), (1,)), ((), ())),
            preferred_element_type=jnp.float32,
        ).astype(jnp.bfloat16)


def project(blocks, vectors, w):
    shape = jax.ShapeDtypeStruct((3 * HEAD_DIM, HALF), jnp.bfloat16)
    return pl.pallas_call(
        project_kernel,
        out_shape=(shape, shape),
        in_specs=whole(10),
        out_specs=tuple(whole(2)),
        scratch_shapes=[pltpu.VMEM((HALF, FEATURES), jnp.bfloat16)],
        compiler_params=params(),
        name="norm_project",
        cost_estimate=pl.CostEstimate(
            flops=2 * HALF * FEATURES * 384, bytes_accessed=2 * 2**20, transcendentals=HALF
        ),
    )(*blocks, vectors, w)


def join_kernel(keep, taken, q_ref, kv_ref):
    for ref, columns in ((keep, slice(0, HALF)), (taken, slice(HALF, 2 * HALF))):
        q_ref[:, columns] = ref[0:HEAD_DIM, :]
        kv_ref[:, columns] = ref[HEAD_DIM:, :]


def join(keep, taken):
    return pl.pallas_call(
        join_kernel,
        out_shape=(
            jax.ShapeDtypeStruct((HEAD_DIM, 2 * HALF), jnp.bfloat16),
            jax.ShapeDtypeStruct((2 * HEAD_DIM, 2 * HALF), jnp.bfloat16),
        ),
        in_specs=whole(2),
        out_specs=tuple(whole(2)),
        compiler_params=params(),
        name="join",
    )(keep, taken)


def attend_kernel(*refs, blocks, sets, work, fresh, pack):
    kv = refs[:blocks]
    queries = refs[blocks : blocks + sets]
    at = blocks + sets
    old = None
    if not fresh:
        old = refs[at : at + 3 * sets]
        at += 3 * sets
    new = None
    packs = refs[at : at + len(pack)]
    at += len(pack)
    if len(pack) < BLOCK // TILE:
        new = refs[at : at + 3 * sets]
        at += 3 * sets
    k_ref, s_ref = refs[at:]
    for b in range(blocks):
        k_ref[b * BLOCK : (b + 1) * BLOCK, :] = kv[b][0:HEAD_DIM, :].T

    steps = [
        (which, b, n == 0, n == len(chosen) - 1)
        for which, chosen in work
        for n, b in enumerate(chosen)
    ]
    tiles = BLOCK // TILE

    def score(step, columns, slot):
        which, b = step[:2]
        s = jnp.dot(
            k_ref[b * BLOCK : (b + 1) * BLOCK, :],
            queries[which][:, columns],
            preferred_element_type=jnp.float32,
        )
        s_ref[slot] = s
        return jnp.max(s, axis=0, keepdims=True)

    def one_tile(columns, next_columns, top, slot, packed):
        for n, (which, b, first, last) in enumerate(steps):
            if first:
                if fresh:
                    m = jnp.full((1, TILE), -jnp.inf, jnp.float32)
                    l = jnp.zeros((1, TILE), jnp.float32)
                    acc = jnp.zeros((HEAD_DIM, TILE), jnp.float32)
                else:
                    m, l, acc = (old[3 * which + i][:, columns] for i in range(3))
            newest = jnp.maximum(m, top)
            factor = jnp.exp2((m - newest) * SCORE_SCALE)
            if n + 1 < len(steps):
                top = score(steps[n + 1], columns, 1 - slot)
            elif next_columns is not None:
                top = score(steps[0], next_columns, 1 - slot)
            weights = jnp.exp2((s_ref[slot] - newest) * SCORE_SCALE)
            slot = 1 - slot
            l = l * factor + jnp.sum(weights, axis=0, keepdims=True)
            acc = acc * factor + jnp.dot(
                kv[b][HEAD_DIM:, :],
                weights.astype(jnp.bfloat16),
                preferred_element_type=jnp.float32,
            )
            m = newest
            if last and packed is None:
                new[3 * which][:, columns] = m
                new[3 * which + 1][:, columns] = l
                new[3 * which + 2][:, columns] = acc
            elif last:
                packed[0:HEAD_DIM, :] = (acc / l).astype(jnp.bfloat16)
                lse = m * SCORE_SCALE + jnp.log2(l)
                high = lse.astype(jnp.bfloat16).astype(jnp.float32)
                middle = (lse - high).astype(jnp.bfloat16).astype(jnp.float32)
                low = lse - high - middle
                row = lax.broadcasted_iota(jnp.int32, (PACK_ROWS - HEAD_DIM, TILE), 0)
                rows = jnp.where(row == 0, high, jnp.where(row == 1, middle, low))
                packed[HEAD_DIM:PACK_ROWS, :] = rows.astype(jnp.bfloat16)
        return top, slot

    if len(steps) % 2 == 0 and len(steps) > 2:

        def body(i, top):
            here = pl.ds(pl.multiple_of(i * TILE, TILE), TILE)
            after = pl.ds(pl.multiple_of(lax.rem(i + 1, tiles) * TILE, TILE), TILE)
            return one_tile(here, after, top, 0, None)[0]

        lax.fori_loop(0, tiles, body, score(steps[0], slice(0, TILE), 0))
    else:
        top, slot = score(steps[0], slice(0, TILE), 0), 0
        for i in range(tiles):
            here = slice(i * TILE, (i + 1) * TILE)
            after = slice((i + 1) * TILE, (i + 2) * TILE) if i + 1 < tiles else None
            packed = packs[pack.index(i)] if i in pack else None
            top, slot = one_tile(here, after, top, slot, packed)


def attend(kv, queries, states, work, pack=()):
    sets = len(queries)
    fresh = states is None
    width = BLOCK if not pack else TILE
    out_shape = [jax.ShapeDtypeStruct((PACK_ROWS, TILE), jnp.bfloat16)] * len(pack)
    if len(pack) < BLOCK // TILE:
        out_shape += [
            jax.ShapeDtypeStruct((1, width), jnp.float32),
            jax.ShapeDtypeStruct((1, width), jnp.float32),
            jax.ShapeDtypeStruct((HEAD_DIM, width), jnp.float32),
        ] * sets
    operands = list(kv) + list(queries) + ([] if fresh else list(states))
    count = sum(len(chosen) for _, chosen in work)
    return pl.pallas_call(
        functools.partial(
            attend_kernel, blocks=len(kv), sets=sets, work=work, fresh=fresh, pack=pack
        ),
        out_shape=tuple(out_shape),
        in_specs=whole(len(operands)),
        out_specs=tuple(whole(len(out_shape))),
        scratch_shapes=[
            pltpu.VMEM((len(kv) * BLOCK, HEAD_DIM), jnp.bfloat16),
            pltpu.VMEM((2, BLOCK, TILE), jnp.float32),
        ],
        compiler_params=params(),
        name="attend",
        cost_estimate=pl.CostEstimate(
            flops=count * 4 * BLOCK * BLOCK * HEAD_DIM * 4,
            bytes_accessed=2**20,
            transcendentals=count * BLOCK * BLOCK,
        ),
    )(*operands)


def unpack(pack_ref):
    split = pack_ref[HEAD_DIM:PACK_ROWS, :].astype(jnp.float32)
    return pack_ref[0:HEAD_DIM, :].astype(jnp.float32), split[0:1] + split[1:2] + split[2:3]


def merge(first, first_lse, second, second_lse):
    top = jnp.maximum(first_lse, second_lse)
    a = jnp.exp2(first_lse - top)
    b = jnp.exp2(second_lse - top)
    inverse = 1.0 / (a + b)
    return (first * (a * inverse) + second * (b * inverse)).astype(jnp.bfloat16)


def output_kernel(m_ref, l_ref, acc_ref, mine_ref, core_ref, diagonal_ref, w_ref, *out_refs):
    total = l_ref[...]
    here = merge(
        acc_ref[...] / total, m_ref[...] * SCORE_SCALE + jnp.log2(total), *unpack(mine_ref)
    )
    other = merge(*unpack(core_ref), *unpack(diagonal_ref))
    attended = jnp.concatenate([here, other], axis=0).T
    width = out_refs[0].shape[1]
    for n, out_ref in enumerate(out_refs):
        out_ref[...] = jnp.dot(
            attended,
            w_ref[:, n * width : (n + 1) * width],
            preferred_element_type=jnp.float32,
        ).astype(jnp.bfloat16)


def output(state, mine, core, diagonal, w_out):
    shape = jax.ShapeDtypeStruct((HALF, FEATURES // len(STEPS)), jnp.bfloat16)
    return pl.pallas_call(
        output_kernel,
        out_shape=(shape,) * len(STEPS),
        in_specs=whole(7),
        out_specs=tuple(whole(len(STEPS))),
        compiler_params=params(),
        name="output_project",
    )(*state, mine, core, diagonal, w_out)


def add_kernel(*refs):
    total = refs[0][...].astype(jnp.float32)
    for ref in refs[1:-1]:
        total = total + ref[...].astype(jnp.float32)
    refs[-1][...] = total.astype(jnp.bfloat16)


def add(*terms):
    return pl.pallas_call(
        add_kernel,
        out_shape=jax.ShapeDtypeStruct(terms[0].shape, jnp.bfloat16),
        in_specs=whole(len(terms)),
        out_specs=whole(1)[0],
        compiler_params=params(),
        name="add",
    )(*terms)


def finish_kernel(tokens_ref, vectors_ref, *refs):
    out_ref = refs[-1]
    total = refs[0][...].astype(jnp.float32)
    for part_ref in refs[1:-1]:
        total = total + part_ref[...].astype(jnp.float32)
    scale = vectors_ref[2 * len(STEPS) : 2 * len(STEPS) + 1, :]
    out_ref[...] = (tokens_ref[...].astype(jnp.float32) + scale * total).astype(jnp.bfloat16)


def finish(parts, tokens, vectors):
    return pl.pallas_call(
        finish_kernel,
        out_shape=jax.ShapeDtypeStruct(tokens.shape, jnp.bfloat16),
        in_specs=whole(2 + len(parts)),
        out_specs=whole(1)[0],
        compiler_params=params(),
        name="finish",
    )(tokens, vectors, *parts)


def per_device(tokens, norm_gain, norm_bias, w_query, w_key, w_value, w_out, layer_scale):
    groups = lax.axis_size("heads")
    width = FEATURES // groups
    core = lax.axis_index("frames") % CORE
    x, y = lax.axis_index("heads") // Y_LO, lax.axis_index("heads") % Y_LO
    sources = [((x - dx) % X) * Y_LO + (y ^ dy) for dx, dy in STEPS]
    targets = [((x + dx) % X) * Y_LO + (y ^ dy) for dx, dy in STEPS]
    place = jnp.stack([core, *sources, *targets]).astype(jnp.int32)

    across = send_heads(tokens, (2, 0))
    beside = send_heads(tokens, (0, 1))
    blocks = [tokens, beside, send_heads(tokens, (1, 0)), send_heads(tokens, (3, 0)), across]
    blocks += [send_heads(beside, (1, 0)), send_heads(beside, (3, 0)), send_heads(across, (0, 1))]
    w_all, w_last, vectors = prepare(
        place,
        w_query,
        w_key,
        w_value,
        w_out,
        norm_gain.reshape(groups, width),
        norm_bias.reshape(groups, width),
        layer_scale.reshape(1, width),
    )
    keep, give = project(blocks, vectors, w_all)
    queries, own = join(keep, send(give, 0, 0, 1))
    right, left = own, own
    mine, theirs = None, None
    for step in range(4):
        near = (right, left)
        right = send(right, 0, 1, 0)
        if step < 3:
            left = send(left, 0, -1, 0)
        if step == 0:
            partner = send(queries, 1, 0, 0)
            mine = attend([own], [queries], None, ((0, (0,)),))
        elif step == 1:
            late = near[1]
            theirs = attend([own, *near], [partner], None, ((0, (0, 1, 2)),))
            mine = attend(near[:1], [queries], mine, ((0, (0,)),))
        else:
            both = attend(
                near, [queries, partner], mine + theirs, ((0, (0, 1)), (1, (0, 1)))
            )
            mine, theirs = both[:3], both[3:]
    for_mine, for_other = attend([right], [partner], theirs, ((0, (0,)),), pack=(0, 1))
    from_partner = send(for_mine, 1, 0, 0)
    from_diagonal = send(for_other, 1, 0, 1)
    for_core, *state = attend([late, right], [queries], mine, ((0, (0, 1)),), pack=(1,))
    from_core = send(for_core, 0, 0, 1)
    terms = dict(zip(STEPS, output(state, from_partner, from_core, from_diagonal, w_last)))
    by_partner = send_heads(terms[2, 1], (0, 1))
    by_column = [send_heads(terms[1, 1], (1, 0)), send_heads(terms[3, 1], (3, 0))]
    parts = [send_heads(add(terms[2, 0], by_partner), (2, 0))]
    parts += [send_heads(add(terms[0, 1], *by_column), (0, 1))]
    parts += [send_heads(terms[1, 0], (1, 0)), send_heads(terms[3, 0], (3, 0)), terms[0, 0]]
    return finish(parts, tokens, vectors)


def solution(mesh):
    in_specs = (
        P("frames", "heads"),
        P(),
        P(),
        P(None, "heads"),
        P(None, "heads"),
        P(None, "heads"),
        P("heads", None),
        P("heads"),
    )
    out_specs = P("frames", "heads")
    return jax.shard_map(
        per_device, mesh=mesh, in_specs=in_specs, out_specs=out_specs, check_vma=False
    )
```

```python
import functools

import jax
import jax.numpy as jnp
from jax import lax
from jax.experimental import pallas as pl
from jax.experimental.pallas import tpu as pltpu
from jax.sharding import PartitionSpec as P

HEAD_DIM = 64
HALF = 512
BLOCK = 1024
TILE = 512
FEATURES = 1024
LOG2E = 1.4426950408889634
SCORE_SCALE = HEAD_DIM ** (-0.5) * LOG2E
PACK_ROWS = 80

Y_HI, Z, CORE = 2, 8, 2


def frames_shift(dy, dz, dc):
    pairs = []
    for y in range(Y_HI):
        for z in range(Z):
            for c in range(CORE):
                source = (y * Z + z) * CORE + c
                target = ((y ^ dy) * Z + (z + dz) % Z) * CORE + (c ^ dc)
                pairs.append((source, target))
    return pairs


def send(array, dy, dz, dc):
    return lax.ppermute(array, "frames", frames_shift(dy, dz, dc))


X, Y_LO = 4, 2
STEPS = ((0, 0), (0, 1), (1, 0), (3, 0), (2, 0), (1, 1), (3, 1), (2, 1))


def heads_shift(dx, dy):
    return [
        (x * Y_LO + y, ((x + dx) % X) * Y_LO + (y ^ dy)) for x in range(X) for y in range(Y_LO)
    ]


def send_heads(array, step):
    return lax.ppermute(array, "heads", heads_shift(*step))


def params(limit=48):
    return pltpu.CompilerParams(vmem_limit_bytes=limit * 2**20)


def whole(count):
    return [pl.BlockSpec(memory_space=pltpu.VMEM)] * count


def prepare_kernel(
    place_ref, wq_hbm, wk_hbm, wv_hbm, w_out_hbm, gain_hbm, bias_hbm, scale_hbm,
    w_ref, out_ref, vectors_ref,
    wq_ref, wk_ref, wv_ref, w_out_ref, gain_ref, bias_ref, scale_ref, flipped_ref, done,
):
    pairs = (
        (wq_hbm, wq_ref), (wk_hbm, wk_ref), (wv_hbm, wv_ref), (w_out_hbm, w_out_ref),
        (gain_hbm, gain_ref), (bias_hbm, bias_ref), (scale_hbm, scale_ref),
    )
    copies = [pltpu.make_async_copy(a, b, done.at[n]) for n, (a, b) in enumerate(pairs)]
    for copy in copies:
        copy.start()
    for copy in copies:
        copy.wait()
    core = place_ref[0]
    heads = [pl.ds(pl.multiple_of(h * HEAD_DIM, HEAD_DIM), HEAD_DIM) for h in (core, 1 - core)]
    count = len(STEPS)
    width = FEATURES // count

    def columns(n):
        return pl.ds(pl.multiple_of(place_ref[n] * width, width), width)

    for k, ref in enumerate((wq_ref, wk_ref, wv_ref)):
        flipped_ref[...] = ref[...].T
        for h, rows in enumerate(heads):
            at = (3 * h + k) * HEAD_DIM
            for n in range(count):
                w_ref[at : at + HEAD_DIM, n * width : (n + 1) * width] = flipped_ref[
                    rows, columns(1 + n)
                ]
    for h, rows in enumerate(heads):
        for n in range(count):
            out_ref[h * HEAD_DIM : (h + 1) * HEAD_DIM, n * width : (n + 1) * width] = w_out_ref[
                rows, columns(1 + count + n)
            ]
    for n in range(count):
        j = place_ref[1 + n]
        vectors_ref[n : n + 1, :] = gain_ref[pl.ds(j, 1), :]
        vectors_ref[count + n : count + n + 1, :] = bias_ref[pl.ds(j, 1), :]
    vectors_ref[2 * count : 3 * count, :] = jnp.broadcast_to(scale_ref[...], (count, width))


def prepare(place, wq, wk, wv, w_out, gain, bias, scale):
    return pl.pallas_call(
        prepare_kernel,
        out_shape=(
            jax.ShapeDtypeStruct((6 * HEAD_DIM, FEATURES), jnp.bfloat16),
            jax.ShapeDtypeStruct((2 * HEAD_DIM, FEATURES), jnp.bfloat16),
            jax.ShapeDtypeStruct((3 * len(STEPS), FEATURES // len(STEPS)), jnp.float32),
        ),
        in_specs=[pl.BlockSpec(memory_space=pltpu.SMEM)]
        + [pl.BlockSpec(memory_space=pltpu.MemorySpace.HBM)] * 7,
        out_specs=tuple(whole(3)),
        scratch_shapes=[
            pltpu.VMEM(a.shape, a.dtype) for a in (wq, wk, wv, w_out, gain, bias, scale)
        ]
        + [pltpu.VMEM((2 * HEAD_DIM, FEATURES), jnp.bfloat16), pltpu.SemaphoreType.DMA((7,))],
        compiler_params=params(),
        name="prepare",
        cost_estimate=pl.CostEstimate(
            flops=2 * HALF * FEATURES * 384, bytes_accessed=4 * 2**20, transcendentals=0
        ),
    )(place, wq, wk, wv, w_out, gain, bias, scale)


def project_kernel(*refs):
    x_refs = refs[:8]
    vectors_ref, w_ref, keep, give, normed_ref = refs[8:]
    count = len(x_refs)
    width = x_refs[0].shape[1]
    total = jnp.zeros((HALF, width), jnp.float32)
    for x_ref in x_refs:
        total = total + x_ref[...].astype(jnp.float32)
    mean = jnp.sum(total, axis=1, keepdims=True) * (1.0 / FEATURES)
    squares = jnp.zeros((HALF, width), jnp.float32)
    for x_ref in x_refs:
        centred = x_ref[...].astype(jnp.float32) - mean
        squares = squares + centred * centred
    variance = jnp.sum(squares, axis=1, keepdims=True) * (1.0 / FEATURES)
    inverse = lax.rsqrt(variance + 1e-06)
    for n, x_ref in enumerate(x_refs):
        centred = x_ref[...].astype(jnp.float32) - mean
        gain = vectors_ref[n : n + 1, :]
        bias = vectors_ref[count + n : count + n + 1, :]
        normed = centred * inverse * gain + bias
        normed_ref[:, n * width : (n + 1) * width] = normed.astype(jnp.bfloat16)
    for h, out in enumerate((keep, give)):
        out[...] = lax.dot_general(
            w_ref[h * 3 * HEAD_DIM : (h + 1) * 3 * HEAD_DIM, :],
            normed_ref[...],
            (((1,), (1,)), ((), ())),
            preferred_element_type=jnp.float32,
        ).astype(jnp.bfloat16)


def project(blocks, vectors, w):
    shape = jax.ShapeDtypeStruct((3 * HEAD_DIM, HALF), jnp.bfloat16)
    return pl.pallas_call(
        project_kernel,
        out_shape=(shape, shape),
        in_specs=whole(10),
        out_specs=tuple(whole(2)),
        scratch_shapes=[pltpu.VMEM((HALF, FEATURES), jnp.bfloat16)],
        compiler_params=params(),
        name="norm_project",
        cost_estimate=pl.CostEstimate(
            flops=2 * HALF * FEATURES * 384, bytes_accessed=2 * 2**20, transcendentals=HALF
        ),
    )(*blocks, vectors, w)


def join_kernel(keep, taken, q_ref, kv_ref):
    for ref, columns in ((keep, slice(0, HALF)), (taken, slice(HALF, 2 * HALF))):
        q_ref[:, columns] = ref[0:HEAD_DIM, :]
        kv_ref[:, columns] = ref[HEAD_DIM:, :]


def join(keep, taken):
    return pl.pallas_call(
        join_kernel,
        out_shape=(
            jax.ShapeDtypeStruct((HEAD_DIM, 2 * HALF), jnp.bfloat16),
            jax.ShapeDtypeStruct((2 * HEAD_DIM, 2 * HALF), jnp.bfloat16),
        ),
        in_specs=whole(2),
        out_specs=tuple(whole(2)),
        compiler_params=params(),
        name="join",
    )(keep, taken)


def attend_kernel(*refs, blocks, sets, work, fresh, pack):
    kv = refs[:blocks]
    queries = refs[blocks : blocks + sets]
    at = blocks + sets
    old = {}
    for which in range(sets):
        if which not in fresh:
            old[which] = refs[at : at + 3]
            at += 3
    k_ref, s_ref = refs[-2:]
    packs, new = refs[at : at + len(pack)], refs[at + len(pack) : -2]
    for b in range(blocks):
        k_ref[b * BLOCK : (b + 1) * BLOCK, :] = kv[b][0:HEAD_DIM, :].T

    steps = [
        (which, b, n == 0, n == len(chosen) - 1)
        for which, chosen in work
        for n, b in enumerate(chosen)
    ]
    tiles = BLOCK // TILE

    def score(step, columns, slot):
        which, b = step[:2]
        s = jnp.dot(
            k_ref[b * BLOCK : (b + 1) * BLOCK, :],
            queries[which][:, columns],
            preferred_element_type=jnp.float32,
        )
        s_ref[slot] = s
        return jnp.max(s, axis=0, keepdims=True)

    def one_tile(tile, columns, next_columns, top, slot):
        for n, (which, b, first, last) in enumerate(steps):
            if first:
                if which in fresh:
                    m = jnp.full((1, TILE), -jnp.inf, jnp.float32)
                    l = jnp.zeros((1, TILE), jnp.float32)
                    acc = jnp.zeros((HEAD_DIM, TILE), jnp.float32)
                else:
                    m, l, acc = (ref[:, columns] for ref in old[which])
            newest = jnp.maximum(m, top)
            factor = jnp.exp2((m - newest) * SCORE_SCALE)
            if n + 1 < len(steps):
                top = score(steps[n + 1], columns, 1 - slot)
            elif next_columns is not None:
                top = score(steps[0], next_columns, 1 - slot)
            weights = jnp.exp2((s_ref[slot] - newest) * SCORE_SCALE)
            slot = 1 - slot
            l = l * factor + jnp.sum(weights, axis=0, keepdims=True)
            acc = acc * factor + jnp.dot(
                kv[b][HEAD_DIM:, :],
                weights.astype(jnp.bfloat16),
                preferred_element_type=jnp.float32,
            )
            m = newest
            if last and tile not in pack:
                new[3 * which][:, columns] = m
                new[3 * which + 1][:, columns] = l
                new[3 * which + 2][:, columns] = acc
            elif last:
                pack_ref = packs[pack.index(tile)]
                pack_ref[0:HEAD_DIM, :] = (acc / l).astype(jnp.bfloat16)
                lse = m * SCORE_SCALE + jnp.log2(l)
                high = lse.astype(jnp.bfloat16).astype(jnp.float32)
                middle = (lse - high).astype(jnp.bfloat16).astype(jnp.float32)
                low = lse - high - middle
                row = lax.broadcasted_iota(jnp.int32, (PACK_ROWS - HEAD_DIM, TILE), 0)
                rows = jnp.where(row == 0, high, jnp.where(row == 1, middle, low))
                pack_ref[HEAD_DIM:PACK_ROWS, :] = rows.astype(jnp.bfloat16)
        return top, slot

    if len(steps) % 2 == 0 and not pack:

        def body(i, top):
            here = pl.ds(pl.multiple_of(i * TILE, TILE), TILE)
            after = pl.ds(pl.multiple_of(lax.rem(i + 1, tiles) * TILE, TILE), TILE)
            return one_tile(-1, here, after, top, 0)[0]

        lax.fori_loop(0, tiles, body, score(steps[0], slice(0, TILE), 0))
    else:
        top, slot = score(steps[0], slice(0, TILE), 0), 0
        for i in range(tiles):
            here = slice(i * TILE, (i + 1) * TILE)
            after = slice((i + 1) * TILE, (i + 2) * TILE) if i + 1 < tiles else None
            top, slot = one_tile(i, here, after, top, slot)


def attend(kv, queries, states, work, pack=()):
    sets = len(queries)
    fresh = tuple(n for n, state in enumerate(states) if state is None)
    width = BLOCK - TILE * len(pack)
    out_shape = [jax.ShapeDtypeStruct((PACK_ROWS, TILE), jnp.bfloat16)] * len(pack)
    if width > 0:
        out_shape += [
            jax.ShapeDtypeStruct((1, width), jnp.float32),
            jax.ShapeDtypeStruct((1, width), jnp.float32),
            jax.ShapeDtypeStruct((HEAD_DIM, width), jnp.float32),
        ] * sets
    operands = list(kv) + list(queries)
    for state in states:
        operands += [] if state is None else list(state)
    count = sum(len(chosen) for _, chosen in work)
    return pl.pallas_call(
        functools.partial(
            attend_kernel, blocks=len(kv), sets=sets, work=work, fresh=fresh, pack=pack
        ),
        out_shape=tuple(out_shape),
        in_specs=whole(len(operands)),
        out_specs=tuple(whole(len(out_shape))),
        scratch_shapes=[
            pltpu.VMEM((len(kv) * BLOCK, HEAD_DIM), jnp.bfloat16),
            pltpu.VMEM((2, BLOCK, TILE), jnp.float32),
        ],
        compiler_params=params(),
        name="attend",
        cost_estimate=pl.CostEstimate(
            flops=count * 4 * BLOCK * BLOCK * HEAD_DIM * 4,
            bytes_accessed=2**20,
            transcendentals=count * BLOCK * BLOCK,
        ),
    )(*operands)


def unpack(pack_ref):
    split = pack_ref[HEAD_DIM:PACK_ROWS, :].astype(jnp.float32)
    return pack_ref[0:HEAD_DIM, :].astype(jnp.float32), split[0:1] + split[1:2] + split[2:3]


def merge(first, first_lse, second, second_lse):
    top = jnp.maximum(first_lse, second_lse)
    a = jnp.exp2(first_lse - top)
    b = jnp.exp2(second_lse - top)
    inverse = 1.0 / (a + b)
    return (first * (a * inverse) + second * (b * inverse)).astype(jnp.bfloat16)


def output_kernel(m_ref, l_ref, acc_ref, mine_ref, core_ref, diagonal_ref, w_ref, *out_refs):
    total = l_ref[...]
    here = merge(
        acc_ref[...] / total, m_ref[...] * SCORE_SCALE + jnp.log2(total), *unpack(mine_ref)
    )
    other = merge(*unpack(core_ref), *unpack(diagonal_ref))
    attended = jnp.concatenate([here, other], axis=0).T
    width = out_refs[0].shape[1]
    for n, out_ref in enumerate(out_refs):
        out_ref[...] = jnp.dot(
            attended,
            w_ref[:, n * width : (n + 1) * width],
            preferred_element_type=jnp.float32,
        ).astype(jnp.bfloat16)


def output(state, mine, core, diagonal, w_out):
    shape = jax.ShapeDtypeStruct((HALF, FEATURES // len(STEPS)), jnp.bfloat16)
    return pl.pallas_call(
        output_kernel,
        out_shape=(shape,) * len(STEPS),
        in_specs=whole(7),
        out_specs=tuple(whole(len(STEPS))),
        compiler_params=params(),
        name="output_project",
    )(*state, mine, core, diagonal, w_out)


def add_kernel(*refs):
    total = refs[0][...].astype(jnp.float32)
    for ref in refs[1:-1]:
        total = total + ref[...].astype(jnp.float32)
    refs[-1][...] = total.astype(jnp.bfloat16)


def add(*terms):
    return pl.pallas_call(
        add_kernel,
        out_shape=jax.ShapeDtypeStruct(terms[0].shape, jnp.bfloat16),
        in_specs=whole(len(terms)),
        out_specs=whole(1)[0],
        compiler_params=params(),
        name="add",
    )(*terms)


def finish_kernel(tokens_ref, vectors_ref, *refs):
    out_ref = refs[-1]
    total = refs[0][...].astype(jnp.float32)
    for part_ref in refs[1:-1]:
        total = total + part_ref[...].astype(jnp.float32)
    scale = vectors_ref[2 * len(STEPS) : 2 * len(STEPS) + 1, :]
    out_ref[...] = (tokens_ref[...].astype(jnp.float32) + scale * total).astype(jnp.bfloat16)


def finish(parts, tokens, vectors):
    return pl.pallas_call(
        finish_kernel,
        out_shape=jax.ShapeDtypeStruct(tokens.shape, jnp.bfloat16),
        in_specs=whole(2 + len(parts)),
        out_specs=whole(1)[0],
        compiler_params=params(),
        name="finish",
    )(tokens, vectors, *parts)


def per_device(tokens, norm_gain, norm_bias, w_query, w_key, w_value, w_out, layer_scale):
    groups = lax.axis_size("heads")
    width = FEATURES // groups
    core = lax.axis_index("frames") % CORE
    x, y = lax.axis_index("heads") // Y_LO, lax.axis_index("heads") % Y_LO
    sources = [((x - dx) % X) * Y_LO + (y ^ dy) for dx, dy in STEPS]
    targets = [((x + dx) % X) * Y_LO + (y ^ dy) for dx, dy in STEPS]
    place = jnp.stack([core, *sources, *targets]).astype(jnp.int32)

    across = send_heads(tokens, (2, 0))
    beside = send_heads(tokens, (0, 1))
    blocks = [tokens, beside, send_heads(tokens, (1, 0)), send_heads(tokens, (3, 0)), across]
    blocks += [send_heads(beside, (1, 0)), send_heads(beside, (3, 0)), send_heads(across, (0, 1))]
    w_all, w_last, vectors = prepare(
        place,
        w_query,
        w_key,
        w_value,
        w_out,
        norm_gain.reshape(groups, width),
        norm_bias.reshape(groups, width),
        layer_scale.reshape(1, width),
    )
    keep, give = project(blocks, vectors, w_all)
    queries, own = join(keep, send(give, 0, 0, 1))
    right, left = own, own
    mine, theirs = None, None
    for step in range(4):
        near = (right, left)
        right = send(right, 0, 1, 0)
        if step < 3:
            left = send(left, 0, -1, 0)
        if step == 0:
            partner = send(queries, 1, 0, 0)
            mine = attend([own], [queries], [None], ((0, (0,)),))
        else:
            if step == 1:
                late = near[1]
                blocks, work = (own, *near), ((1, (0, 1, 2)), (0, (1,)))
            else:
                blocks, work = near, ((0, (0, 1)), (1, (0, 1)))
            both = attend(blocks, [queries, partner], [mine, theirs], work)
            mine, theirs = both[:3], both[3:]
    for_mine, for_other = attend([right], [partner], [theirs], ((0, (0,)),), pack=(0, 1))
    from_partner = send(for_mine, 1, 0, 0)
    from_diagonal = send(for_other, 1, 0, 1)
    for_core, *state = attend([late, right], [queries], [mine], ((0, (0, 1)),), pack=(1,))
    from_core = send(for_core, 0, 0, 1)
    terms = dict(zip(STEPS, output(state, from_partner, from_core, from_diagonal, w_last)))
    by_column = [send_heads(terms[1, 1], (1, 0)), send_heads(terms[3, 1], (3, 0))]
    parts = [send_heads(add(terms[0, 1], *by_column), (0, 1))]
    by_partner = send_heads(terms[2, 1], (0, 1))
    parts += [send_heads(add(terms[2, 0], by_partner), (2, 0))]
    parts += [send_heads(terms[1, 0], (1, 0)), send_heads(terms[3, 0], (3, 0)), terms[0, 0]]
    return finish(parts, tokens, vectors)


def solution(mesh):
    in_specs = (
        P("frames", "heads"),
        P(),
        P(),
        P(None, "heads"),
        P(None, "heads"),
        P(None, "heads"),
        P("heads", None),
        P("heads"),
    )
    out_specs = P("frames", "heads")
    return jax.shard_map(
        per_device, mesh=mesh, in_specs=in_specs, out_specs=out_specs, check_vma=False
    )
```

```python
import functools

import jax
import jax.numpy as jnp
from jax import lax
from jax.experimental import pallas as pl
from jax.experimental.pallas import tpu as pltpu
from jax.sharding import PartitionSpec as P

HEAD_DIM = 64
HALF = 512
BLOCK = 1024
TILE = 512
FEATURES = 1024
LOG2E = 1.4426950408889634
SCORE_SCALE = HEAD_DIM ** (-0.5) * LOG2E
PACK_ROWS = 80

Y_HI, Z, CORE = 2, 8, 2


def frames_shift(dy, dz, dc):
    pairs = []
    for y in range(Y_HI):
        for z in range(Z):
            for c in range(CORE):
                source = (y * Z + z) * CORE + c
                target = ((y ^ dy) * Z + (z + dz) % Z) * CORE + (c ^ dc)
                pairs.append((source, target))
    return pairs


def send(array, dy, dz, dc):
    return lax.ppermute(array, "frames", frames_shift(dy, dz, dc))


X, Y_LO = 4, 2
STEPS = ((0, 0), (0, 1), (1, 0), (3, 0), (2, 0), (1, 1), (3, 1), (2, 1))


def heads_shift(dx, dy):
    return [
        (x * Y_LO + y, ((x + dx) % X) * Y_LO + (y ^ dy)) for x in range(X) for y in range(Y_LO)
    ]


def send_heads(array, step):
    return lax.ppermute(array, "heads", heads_shift(*step))


def params(limit=48):
    return pltpu.CompilerParams(vmem_limit_bytes=limit * 2**20)


def whole(count):
    return [pl.BlockSpec(memory_space=pltpu.VMEM)] * count


def prepare_kernel(
    place_ref, wq_hbm, wk_hbm, wv_hbm, gain_hbm, bias_hbm,
    w_ref, vectors_ref,
    wq_ref, wk_ref, wv_ref, gain_ref, bias_ref, flipped_ref, done,
):
    pairs = (
        (wq_hbm, wq_ref), (wk_hbm, wk_ref), (wv_hbm, wv_ref),
        (gain_hbm, gain_ref), (bias_hbm, bias_ref),
    )
    copies = [pltpu.make_async_copy(a, b, done.at[n]) for n, (a, b) in enumerate(pairs)]
    for copy in copies:
        copy.start()
    for copy in copies:
        copy.wait()
    core = place_ref[0]
    heads = [pl.ds(pl.multiple_of(h * HEAD_DIM, HEAD_DIM), HEAD_DIM) for h in (core, 1 - core)]
    count = len(STEPS)
    width = FEATURES // count

    def columns(n):
        return pl.ds(pl.multiple_of(place_ref[n] * width, width), width)

    for k, ref in enumerate((wq_ref, wk_ref, wv_ref)):
        flipped_ref[...] = ref[...].T
        for h, rows in enumerate(heads):
            at = (3 * h + k) * HEAD_DIM
            for n in range(count):
                w_ref[at : at + HEAD_DIM, n * width : (n + 1) * width] = flipped_ref[
                    rows, columns(1 + n)
                ]
    for n in range(count):
        j = place_ref[1 + n]
        vectors_ref[n : n + 1, :] = gain_ref[pl.ds(j, 1), :]
        vectors_ref[count + n : count + n + 1, :] = bias_ref[pl.ds(j, 1), :]


def prepare(place, wq, wk, wv, gain, bias):
    return pl.pallas_call(
        prepare_kernel,
        out_shape=(
            jax.ShapeDtypeStruct((6 * HEAD_DIM, FEATURES), jnp.bfloat16),
            jax.ShapeDtypeStruct((2 * len(STEPS), FEATURES // len(STEPS)), jnp.float32),
        ),
        in_specs=[pl.BlockSpec(memory_space=pltpu.SMEM)]
        + [pl.BlockSpec(memory_space=pltpu.MemorySpace.HBM)] * 5,
        out_specs=tuple(whole(2)),
        scratch_shapes=[pltpu.VMEM(a.shape, a.dtype) for a in (wq, wk, wv, gain, bias)]
        + [pltpu.VMEM((2 * HEAD_DIM, FEATURES), jnp.bfloat16), pltpu.SemaphoreType.DMA((5,))],
        compiler_params=params(),
        name="prepare",
        cost_estimate=pl.CostEstimate(
            flops=2 * HALF * FEATURES * 384, bytes_accessed=4 * 2**20, transcendentals=0
        ),
    )(place, wq, wk, wv, gain, bias)


def arrange_kernel(place_ref, w_ref, scale_ref, after_ref, out_ref, vector_ref):
    core = place_ref[0]
    count = len(STEPS)
    width = FEATURES // count
    for at, h in enumerate((core, 1 - core)):
        rows = pl.ds(pl.multiple_of(h * HEAD_DIM, HEAD_DIM), HEAD_DIM)
        for n in range(count):
            columns = pl.ds(pl.multiple_of(place_ref[1 + count + n] * width, width), width)
            out_ref[at * HEAD_DIM : (at + 1) * HEAD_DIM, n * width : (n + 1) * width] = w_ref[
                rows, columns
            ]
    vector_ref[...] = jnp.broadcast_to(scale_ref[...], vector_ref.shape)


def arrange(place, w_out, scale, after):
    return pl.pallas_call(
        arrange_kernel,
        out_shape=(
            jax.ShapeDtypeStruct(w_out.shape, w_out.dtype),
            jax.ShapeDtypeStruct((8, scale.shape[1]), jnp.float32),
        ),
        in_specs=[pl.BlockSpec(memory_space=pltpu.SMEM)]
        + whole(2)
        + [pl.BlockSpec(memory_space=pl.ANY)],
        out_specs=tuple(whole(2)),
        compiler_params=params(),
        name="arrange",
    )(place, w_out, scale, after)


def project_kernel(*refs):
    x_refs = refs[:8]
    vectors_ref, w_ref, keep, give, normed_ref = refs[8:]
    count = len(x_refs)
    width = x_refs[0].shape[1]
    total = jnp.zeros((HALF, width), jnp.float32)
    for x_ref in x_refs:
        total = total + x_ref[...].astype(jnp.float32)
    mean = jnp.sum(total, axis=1, keepdims=True) * (1.0 / FEATURES)
    squares = jnp.zeros((HALF, width), jnp.float32)
    for x_ref in x_refs:
        centred = x_ref[...].astype(jnp.float32) - mean
        squares = squares + centred * centred
    variance = jnp.sum(squares, axis=1, keepdims=True) * (1.0 / FEATURES)
    inverse = lax.rsqrt(variance + 1e-06)
    for n, x_ref in enumerate(x_refs):
        centred = x_ref[...].astype(jnp.float32) - mean
        gain = vectors_ref[n : n + 1, :]
        bias = vectors_ref[count + n : count + n + 1, :]
        normed = centred * inverse * gain + bias
        normed_ref[:, n * width : (n + 1) * width] = normed.astype(jnp.bfloat16)
    for h, out in enumerate((keep, give)):
        out[...] = lax.dot_general(
            w_ref[h * 3 * HEAD_DIM : (h + 1) * 3 * HEAD_DIM, :],
            normed_ref[...],
            (((1,), (1,)), ((), ())),
            preferred_element_type=jnp.float32,
        ).astype(jnp.bfloat16)


def project(blocks, vectors, w):
    shape = jax.ShapeDtypeStruct((3 * HEAD_DIM, HALF), jnp.bfloat16)
    return pl.pallas_call(
        project_kernel,
        out_shape=(shape, shape),
        in_specs=whole(10),
        out_specs=tuple(whole(2)),
        scratch_shapes=[pltpu.VMEM((HALF, FEATURES), jnp.bfloat16)],
        compiler_params=params(),
        name="norm_project",
        cost_estimate=pl.CostEstimate(
            flops=2 * HALF * FEATURES * 384, bytes_accessed=2 * 2**20, transcendentals=HALF
        ),
    )(*blocks, vectors, w)


def join_kernel(keep, taken, q_ref, kv_ref):
    for ref, columns in ((keep, slice(0, HALF)), (taken, slice(HALF, 2 * HALF))):
        q_ref[:, columns] = ref[0:HEAD_DIM, :]
        kv_ref[:, columns] = ref[HEAD_DIM:, :]


def join(keep, taken):
    return pl.pallas_call(
        join_kernel,
        out_shape=(
            jax.ShapeDtypeStruct((HEAD_DIM, 2 * HALF), jnp.bfloat16),
            jax.ShapeDtypeStruct((2 * HEAD_DIM, 2 * HALF), jnp.bfloat16),
        ),
        in_specs=whole(2),
        out_specs=tuple(whole(2)),
        compiler_params=params(),
        name="join",
    )(keep, taken)


def attend_kernel(*refs, blocks, sets, work, fresh, pack, waits):
    kv = refs[:blocks]
    queries = refs[blocks : blocks + sets]
    at = blocks + sets
    old = {}
    for which in range(sets):
        if which not in fresh:
            old[which] = refs[at : at + 3]
            at += 3
    k_ref, s_ref = refs[-2:]
    at += waits
    packs, new = refs[at : at + len(pack)], refs[at + len(pack) : -2]
    for b in range(blocks):
        k_ref[b * BLOCK : (b + 1) * BLOCK, :] = kv[b][0:HEAD_DIM, :].T

    steps = [
        (which, b, n == 0, n == len(chosen) - 1)
        for which, chosen in work
        for n, b in enumerate(chosen)
    ]
    tiles = BLOCK // TILE

    def score(step, columns, slot):
        which, b = step[:2]
        s = jnp.dot(
            k_ref[b * BLOCK : (b + 1) * BLOCK, :],
            queries[which][:, columns],
            preferred_element_type=jnp.float32,
        )
        s_ref[slot] = s
        return jnp.max(s, axis=0, keepdims=True)

    def one_tile(tile, columns, next_columns, top, slot):
        for n, (which, b, first, last) in enumerate(steps):
            if first:
                if which in fresh:
                    m = jnp.full((1, TILE), -jnp.inf, jnp.float32)
                    l = jnp.zeros((1, TILE), jnp.float32)
                    acc = jnp.zeros((HEAD_DIM, TILE), jnp.float32)
                else:
                    m, l, acc = (ref[:, columns] for ref in old[which])
            newest = jnp.maximum(m, top)
            factor = jnp.exp2((m - newest) * SCORE_SCALE)
            if n + 1 < len(steps):
                top = score(steps[n + 1], columns, 1 - slot)
            elif next_columns is not None:
                top = score(steps[0], next_columns, 1 - slot)
            weights = jnp.exp2((s_ref[slot] - newest) * SCORE_SCALE)
            slot = 1 - slot
            l = l * factor + jnp.sum(weights, axis=0, keepdims=True)
            acc = acc * factor + jnp.dot(
                kv[b][HEAD_DIM:, :],
                weights.astype(jnp.bfloat16),
                preferred_element_type=jnp.float32,
            )
            m = newest
            if last and tile not in pack:
                new[3 * which][:, columns] = m
                new[3 * which + 1][:, columns] = l
                new[3 * which + 2][:, columns] = acc
            elif last:
                pack_ref = packs[pack.index(tile)]
                pack_ref[0:HEAD_DIM, :] = (acc / l).astype(jnp.bfloat16)
                lse = m * SCORE_SCALE + jnp.log2(l)
                high = lse.astype(jnp.bfloat16).astype(jnp.float32)
                middle = (lse - high).astype(jnp.bfloat16).astype(jnp.float32)
                low = lse - high - middle
                row = lax.broadcasted_iota(jnp.int32, (PACK_ROWS - HEAD_DIM, TILE), 0)
                rows = jnp.where(row == 0, high, jnp.where(row == 1, middle, low))
                pack_ref[HEAD_DIM:PACK_ROWS, :] = rows.astype(jnp.bfloat16)
        return top, slot

    if len(steps) % 2 == 0 and not pack:

        def body(i, top):
            here = pl.ds(pl.multiple_of(i * TILE, TILE), TILE)
            after = pl.ds(pl.multiple_of(lax.rem(i + 1, tiles) * TILE, TILE), TILE)
            return one_tile(-1, here, after, top, 0)[0]

        lax.fori_loop(0, tiles, body, score(steps[0], slice(0, TILE), 0))
    else:
        top, slot = score(steps[0], slice(0, TILE), 0), 0
        for i in range(tiles):
            here = slice(i * TILE, (i + 1) * TILE)
            after = slice((i + 1) * TILE, (i + 2) * TILE) if i + 1 < tiles else None
            top, slot = one_tile(i, here, after, top, slot)


def attend(kv, queries, states, work, pack=(), after=()):
    sets = len(queries)
    fresh = tuple(n for n, state in enumerate(states) if state is None)
    width = BLOCK - TILE * len(pack)
    out_shape = [jax.ShapeDtypeStruct((PACK_ROWS, TILE), jnp.bfloat16)] * len(pack)
    if width > 0:
        out_shape += [
            jax.ShapeDtypeStruct((1, width), jnp.float32),
            jax.ShapeDtypeStruct((1, width), jnp.float32),
            jax.ShapeDtypeStruct((HEAD_DIM, width), jnp.float32),
        ] * sets
    operands = list(kv) + list(queries)
    for state in states:
        operands += [] if state is None else list(state)
    count = sum(len(chosen) for _, chosen in work)
    return pl.pallas_call(
        functools.partial(
            attend_kernel,
            blocks=len(kv),
            sets=sets,
            work=work,
            fresh=fresh,
            pack=pack,
            waits=len(after),
        ),
        out_shape=tuple(out_shape),
        in_specs=whole(len(operands)) + [pl.BlockSpec(memory_space=pl.ANY)] * len(after),
        out_specs=tuple(whole(len(out_shape))),
        scratch_shapes=[
            pltpu.VMEM((len(kv) * BLOCK, HEAD_DIM), jnp.bfloat16),
            pltpu.VMEM((2, BLOCK, TILE), jnp.float32),
        ],
        compiler_params=params(),
        name="attend",
        cost_estimate=pl.CostEstimate(
            flops=count * 4 * BLOCK * BLOCK * HEAD_DIM * 4,
            bytes_accessed=2**20,
            transcendentals=count * BLOCK * BLOCK,
        ),
    )(*operands, *after)


def unpack(pack_ref):
    split = pack_ref[HEAD_DIM:PACK_ROWS, :].astype(jnp.float32)
    return pack_ref[0:HEAD_DIM, :].astype(jnp.float32), split[0:1] + split[1:2] + split[2:3]


def merge(first, first_lse, second, second_lse):
    top = jnp.maximum(first_lse, second_lse)
    a = jnp.exp2(first_lse - top)
    b = jnp.exp2(second_lse - top)
    inverse = 1.0 / (a + b)
    return (first * (a * inverse) + second * (b * inverse)).astype(jnp.bfloat16)


def output_kernel(m_ref, l_ref, acc_ref, mine_ref, core_ref, diagonal_ref, w_ref, *out_refs):
    total = l_ref[...]
    here = merge(
        acc_ref[...] / total, m_ref[...] * SCORE_SCALE + jnp.log2(total), *unpack(mine_ref)
    )
    other = merge(*unpack(core_ref), *unpack(diagonal_ref))
    attended = jnp.concatenate([here, other], axis=0).T
    width = out_refs[0].shape[1]
    for n, out_ref in enumerate(out_refs):
        out_ref[...] = jnp.dot(
            attended,
            w_ref[:, n * width : (n + 1) * width],
            preferred_element_type=jnp.float32,
        ).astype(jnp.bfloat16)


def output(state, mine, core, diagonal, w_out):
    shape = jax.ShapeDtypeStruct((HALF, FEATURES // len(STEPS)), jnp.bfloat16)
    return pl.pallas_call(
        output_kernel,
        out_shape=(shape,) * len(STEPS),
        in_specs=whole(7),
        out_specs=tuple(whole(len(STEPS))),
        compiler_params=params(),
        name="output_project",
    )(*state, mine, core, diagonal, w_out)


def add_kernel(*refs, terms):
    total = refs[0][...].astype(jnp.float32)
    for ref in refs[1:terms]:
        total = total + ref[...].astype(jnp.float32)
    refs[-1][...] = total.astype(jnp.bfloat16)


def add(*terms, after=()):
    return pl.pallas_call(
        functools.partial(add_kernel, terms=len(terms)),
        out_shape=jax.ShapeDtypeStruct(terms[0].shape, jnp.bfloat16),
        in_specs=whole(len(terms)) + [pl.BlockSpec(memory_space=pl.ANY)] * len(after),
        out_specs=whole(1)[0],
        compiler_params=params(),
        name="add",
    )(*terms, *after)


def finish_kernel(tokens_ref, scale_ref, *refs):
    out_ref = refs[-1]
    total = refs[0][...].astype(jnp.float32)
    for part_ref in refs[1:-1]:
        total = total + part_ref[...].astype(jnp.float32)
    scale = scale_ref[0:1, :]
    out_ref[...] = (tokens_ref[...].astype(jnp.float32) + scale * total).astype(jnp.bfloat16)


def finish(parts, tokens, scale):
    return pl.pallas_call(
        finish_kernel,
        out_shape=jax.ShapeDtypeStruct(tokens.shape, jnp.bfloat16),
        in_specs=whole(2 + len(parts)),
        out_specs=whole(1)[0],
        compiler_params=params(),
        name="finish",
    )(tokens, scale, *parts)


def per_device(tokens, norm_gain, norm_bias, w_query, w_key, w_value, w_out, layer_scale):
    groups = lax.axis_size("heads")
    width = FEATURES // groups
    core = lax.axis_index("frames") % CORE
    x, y = lax.axis_index("heads") // Y_LO, lax.axis_index("heads") % Y_LO
    sources = [((x - dx) % X) * Y_LO + (y ^ dy) for dx, dy in STEPS]
    targets = [((x + dx) % X) * Y_LO + (y ^ dy) for dx, dy in STEPS]
    place = jnp.stack([core, *sources, *targets]).astype(jnp.int32)

    across = send_heads(tokens, (2, 0))
    beside = send_heads(tokens, (0, 1))
    blocks = [tokens, beside, send_heads(tokens, (1, 0)), send_heads(tokens, (3, 0)), across]
    blocks += [send_heads(beside, (1, 0)), send_heads(beside, (3, 0)), send_heads(across, (0, 1))]
    w_all, vectors = prepare(
        place,
        w_query,
        w_key,
        w_value,
        norm_gain.reshape(groups, width),
        norm_bias.reshape(groups, width),
    )
    keep, give = project(blocks, vectors, w_all)
    queries, own = join(keep, send(give, 0, 0, 1))
    w_last, scale = arrange(place, w_out, layer_scale.reshape(1, width), own)
    right, left = own, own
    mine, theirs = None, None
    for step in range(4):
        near = (right, left)
        right = send(right, 0, 1, 0)
        if step < 3:
            left = send(left, 0, -1, 0)
        if step == 0:
            partner = send(queries, 1, 0, 0)
            mine = attend([own], [queries], [None], ((0, (0,)),))
        else:
            if step == 1:
                late = near[1]
                blocks, work = (own, *near), ((1, (0, 1, 2)), (0, (1,)))
            else:
                blocks, work = near, ((0, (0, 1)), (1, (0, 1)))
            both = attend(
                blocks, [queries, partner], [mine, theirs], work, after=[w_last] if step == 1 else ()
            )
            mine, theirs = both[:3], both[3:]
    for_mine, for_other = attend([right], [partner], [theirs], ((0, (0,)),), pack=(0, 1))
    from_partner = send(for_mine, 1, 0, 0)
    from_diagonal = send(for_other, 1, 0, 1)
    for_core, *state = attend(
        [late, right], [queries], [mine], ((0, (0, 1)),), pack=(1,)
    )
    from_core = send(for_core, 0, 0, 1)
    terms = dict(zip(STEPS, output(state, from_partner, from_core, from_diagonal, w_last)))
    by_column = [send_heads(terms[1, 1], (1, 0)), send_heads(terms[3, 1], (3, 0))]
    parts = [send_heads(add(terms[0, 1], *by_column), (0, 1))]
    by_partner = send_heads(terms[2, 1], (0, 1))
    parts += [send_heads(add(terms[2, 0], by_partner), (2, 0))]
    parts += [send_heads(terms[1, 0], (1, 0)), send_heads(terms[3, 0], (3, 0)), terms[0, 0]]
    return finish(parts, tokens, scale)


def solution(mesh):
    in_specs = (
        P("frames", "heads"),
        P(),
        P(),
        P(None, "heads"),
        P(None, "heads"),
        P(None, "heads"),
        P("heads", None),
        P("heads"),
    )
    out_specs = P("frames", "heads")
    return jax.shard_map(
        per_device, mesh=mesh, in_specs=in_specs, out_specs=out_specs, check_vma=False
    )
```

```python
import functools

import jax
import jax.numpy as jnp
from jax import lax
from jax.experimental import pallas as pl
from jax.experimental.pallas import tpu as pltpu
from jax.sharding import PartitionSpec as P

HEAD_DIM = 64
HALF = 512
BLOCK = 1024
TILE = 512
FEATURES = 1024
LOG2E = 1.4426950408889634
SCORE_SCALE = HEAD_DIM ** (-0.5) * LOG2E
PACK_ROWS = 80

Y_HI, Z, CORE = 2, 8, 2


def frames_shift(dy, dz, dc):
    pairs = []
    for y in range(Y_HI):
        for z in range(Z):
            for c in range(CORE):
                source = (y * Z + z) * CORE + c
                target = ((y ^ dy) * Z + (z + dz) % Z) * CORE + (c ^ dc)
                pairs.append((source, target))
    return pairs


def send(array, dy, dz, dc):
    return lax.ppermute(array, "frames", frames_shift(dy, dz, dc))


X, Y_LO = 4, 2
STEPS = ((0, 0), (0, 1), (1, 0), (3, 0), (2, 0), (1, 1), (3, 1), (2, 1))


def heads_shift(dx, dy):
    return [
        (x * Y_LO + y, ((x + dx) % X) * Y_LO + (y ^ dy)) for x in range(X) for y in range(Y_LO)
    ]


def send_heads(array, step):
    return lax.ppermute(array, "heads", heads_shift(*step))


def params(limit=48):
    return pltpu.CompilerParams(vmem_limit_bytes=limit * 2**20)


def whole(count):
    return [pl.BlockSpec(memory_space=pltpu.VMEM)] * count


def prepare_kernel(
    place_ref, wq_hbm, wk_hbm, wv_hbm, gain_hbm, bias_hbm,
    w_ref, vectors_ref,
    wq_ref, wk_ref, wv_ref, gain_ref, bias_ref, flipped_ref, done,
):
    pairs = (
        (wq_hbm, wq_ref), (wk_hbm, wk_ref), (wv_hbm, wv_ref),
        (gain_hbm, gain_ref), (bias_hbm, bias_ref),
    )
    copies = [pltpu.make_async_copy(a, b, done.at[n]) for n, (a, b) in enumerate(pairs)]
    for copy in copies:
        copy.start()
    for copy in copies:
        copy.wait()
    core = place_ref[0]
    heads = [pl.ds(pl.multiple_of(h * HEAD_DIM, HEAD_DIM), HEAD_DIM) for h in (core, 1 - core)]
    count = len(STEPS)
    width = FEATURES // count

    def columns(n):
        return pl.ds(pl.multiple_of(place_ref[n] * width, width), width)

    for k, ref in enumerate((wq_ref, wk_ref, wv_ref)):
        flipped_ref[...] = ref[...].T
        for h, rows in enumerate(heads):
            at = (3 * h + k) * HEAD_DIM
            for n in range(count):
                w_ref[at : at + HEAD_DIM, n * width : (n + 1) * width] = flipped_ref[
                    rows, columns(1 + n)
                ]
    for n in range(count):
        j = place_ref[1 + n]
        vectors_ref[n : n + 1, :] = gain_ref[pl.ds(j, 1), :]
        vectors_ref[count + n : count + n + 1, :] = bias_ref[pl.ds(j, 1), :]


def prepare(place, wq, wk, wv, gain, bias):
    return pl.pallas_call(
        prepare_kernel,
        out_shape=(
            jax.ShapeDtypeStruct((6 * HEAD_DIM, FEATURES), jnp.bfloat16),
            jax.ShapeDtypeStruct((2 * len(STEPS), FEATURES // len(STEPS)), jnp.float32),
        ),
        in_specs=[pl.BlockSpec(memory_space=pltpu.SMEM)]
        + [pl.BlockSpec(memory_space=pltpu.MemorySpace.HBM)] * 5,
        out_specs=tuple(whole(2)),
        scratch_shapes=[pltpu.VMEM(a.shape, a.dtype) for a in (wq, wk, wv, gain, bias)]
        + [pltpu.VMEM((2 * HEAD_DIM, FEATURES), jnp.bfloat16), pltpu.SemaphoreType.DMA((5,))],
        compiler_params=params(),
        name="prepare",
        cost_estimate=pl.CostEstimate(
            flops=2 * HALF * FEATURES * 384, bytes_accessed=4 * 2**20, transcendentals=0
        ),
    )(place, wq, wk, wv, gain, bias)


def arrange_kernel(place_ref, w_ref, scale_ref, after_ref, out_ref, vector_ref):
    core = place_ref[0]
    count = len(STEPS)
    width = FEATURES // count
    for at, h in enumerate((core, 1 - core)):
        rows = pl.ds(pl.multiple_of(h * HEAD_DIM, HEAD_DIM), HEAD_DIM)
        for n in range(count):
            columns = pl.ds(pl.multiple_of(place_ref[1 + count + n] * width, width), width)
            out_ref[at * HEAD_DIM : (at + 1) * HEAD_DIM, n * width : (n + 1) * width] = w_ref[
                rows, columns
            ]
    vector_ref[...] = jnp.broadcast_to(scale_ref[...], vector_ref.shape)


def arrange(place, w_out, scale, after):
    return pl.pallas_call(
        arrange_kernel,
        out_shape=(
            jax.ShapeDtypeStruct(w_out.shape, w_out.dtype),
            jax.ShapeDtypeStruct((8, scale.shape[1]), jnp.float32),
        ),
        in_specs=[pl.BlockSpec(memory_space=pltpu.SMEM)]
        + whole(2)
        + [pl.BlockSpec(memory_space=pl.ANY)],
        out_specs=tuple(whole(2)),
        compiler_params=params(),
        name="arrange",
    )(place, w_out, scale, after)


def project_kernel(*refs):
    x_refs = refs[:8]
    vectors_ref, w_ref, keep, give, normed_ref = refs[8:]
    count = len(x_refs)
    width = x_refs[0].shape[1]
    total = jnp.zeros((HALF, width), jnp.float32)
    for x_ref in x_refs:
        total = total + x_ref[...].astype(jnp.float32)
    mean = jnp.sum(total, axis=1, keepdims=True) * (1.0 / FEATURES)
    squares = jnp.zeros((HALF, width), jnp.float32)
    for x_ref in x_refs:
        centred = x_ref[...].astype(jnp.float32) - mean
        squares = squares + centred * centred
    variance = jnp.sum(squares, axis=1, keepdims=True) * (1.0 / FEATURES)
    inverse = lax.rsqrt(variance + 1e-06)
    for n, x_ref in enumerate(x_refs):
        centred = x_ref[...].astype(jnp.float32) - mean
        gain = vectors_ref[n : n + 1, :]
        bias = vectors_ref[count + n : count + n + 1, :]
        normed = centred * inverse * gain + bias
        normed_ref[:, n * width : (n + 1) * width] = normed.astype(jnp.bfloat16)
    for h, out in enumerate((keep, give)):
        out[...] = lax.dot_general(
            w_ref[h * 3 * HEAD_DIM : (h + 1) * 3 * HEAD_DIM, :],
            normed_ref[...],
            (((1,), (1,)), ((), ())),
            preferred_element_type=jnp.float32,
        ).astype(jnp.bfloat16)


def project(blocks, vectors, w):
    shape = jax.ShapeDtypeStruct((3 * HEAD_DIM, HALF), jnp.bfloat16)
    return pl.pallas_call(
        project_kernel,
        out_shape=(shape, shape),
        in_specs=whole(10),
        out_specs=tuple(whole(2)),
        scratch_shapes=[pltpu.VMEM((HALF, FEATURES), jnp.bfloat16)],
        compiler_params=params(),
        name="norm_project",
        cost_estimate=pl.CostEstimate(
            flops=2 * HALF * FEATURES * 384, bytes_accessed=2 * 2**20, transcendentals=HALF
        ),
    )(*blocks, vectors, w)


def join_kernel(keep, taken, q_ref, kv_ref):
    for ref, columns in ((keep, slice(0, HALF)), (taken, slice(HALF, 2 * HALF))):
        q_ref[:, columns] = ref[0:HEAD_DIM, :]
        kv_ref[:, columns] = ref[HEAD_DIM:, :]


def join(keep, taken):
    return pl.pallas_call(
        join_kernel,
        out_shape=(
            jax.ShapeDtypeStruct((HEAD_DIM, 2 * HALF), jnp.bfloat16),
            jax.ShapeDtypeStruct((2 * HEAD_DIM, 2 * HALF), jnp.bfloat16),
        ),
        in_specs=whole(2),
        out_specs=tuple(whole(2)),
        compiler_params=params(),
        name="join",
    )(keep, taken)


def attend_kernel(*refs, blocks, sets, work, fresh, pack, waits):
    kv = refs[:blocks]
    queries = refs[blocks : blocks + sets]
    at = blocks + sets
    old = {}
    for which in range(sets):
        if which not in fresh:
            old[which] = refs[at : at + 3]
            at += 3
    k_ref, s_ref = refs[-2:]
    at += waits
    packs, new = refs[at : at + len(pack)], refs[at + len(pack) : -2]
    for b in range(blocks):
        k_ref[b * BLOCK : (b + 1) * BLOCK, :] = kv[b][0:HEAD_DIM, :].T

    steps = [
        (which, b, n == 0, n == len(chosen) - 1)
        for which, chosen in work
        for n, b in enumerate(chosen)
    ]
    tiles = BLOCK // TILE

    def score(step, columns, slot):
        which, b = step[:2]
        s = jnp.dot(
            k_ref[b * BLOCK : (b + 1) * BLOCK, :],
            queries[which][:, columns],
            preferred_element_type=jnp.float32,
        )
        s_ref[slot] = s
        return jnp.max(s, axis=0, keepdims=True)

    def one_tile(tile, columns, next_columns, top, slot):
        for n, (which, b, first, last) in enumerate(steps):
            if first:
                if which in fresh:
                    m = jnp.full((1, TILE), -jnp.inf, jnp.float32)
                    l = jnp.zeros((1, TILE), jnp.float32)
                    acc = jnp.zeros((HEAD_DIM, TILE), jnp.float32)
                else:
                    m, l, acc = (ref[:, columns] for ref in old[which])
            newest = jnp.maximum(m, top)
            factor = jnp.exp2((m - newest) * SCORE_SCALE)
            if n + 1 < len(steps):
                top = score(steps[n + 1], columns, 1 - slot)
            elif next_columns is not None:
                top = score(steps[0], next_columns, 1 - slot)
            weights = jnp.exp2((s_ref[slot] - newest) * SCORE_SCALE)
            slot = 1 - slot
            l = l * factor + jnp.sum(weights, axis=0, keepdims=True)
            acc = acc * factor + jnp.dot(
                kv[b][HEAD_DIM:, :],
                weights.astype(jnp.bfloat16),
                preferred_element_type=jnp.float32,
            )
            m = newest
            if last and tile not in pack:
                new[3 * which][:, columns] = m
                new[3 * which + 1][:, columns] = l
                new[3 * which + 2][:, columns] = acc
            elif last:
                pack_ref = packs[pack.index(tile)]
                pack_ref[0:HEAD_DIM, :] = (acc / l).astype(jnp.bfloat16)
                lse = m * SCORE_SCALE + jnp.log2(l)
                high = lse.astype(jnp.bfloat16).astype(jnp.float32)
                middle = (lse - high).astype(jnp.bfloat16).astype(jnp.float32)
                low = lse - high - middle
                row = lax.broadcasted_iota(jnp.int32, (PACK_ROWS - HEAD_DIM, TILE), 0)
                rows = jnp.where(row == 0, high, jnp.where(row == 1, middle, low))
                pack_ref[HEAD_DIM:PACK_ROWS, :] = rows.astype(jnp.bfloat16)
        return top, slot

    if not pack:

        def body(i, top):
            here = pl.ds(pl.multiple_of(i * TILE, TILE), TILE)
            after = pl.ds(pl.multiple_of(lax.rem(i + 1, tiles) * TILE, TILE), TILE)
            slot = 0 if len(steps) % 2 == 0 else lax.rem(i, 2)
            return one_tile(-1, here, after, top, slot)[0]

        lax.fori_loop(0, tiles, body, score(steps[0], slice(0, TILE), 0))
    else:
        top, slot = score(steps[0], slice(0, TILE), 0), 0
        for i in range(tiles):
            here = slice(i * TILE, (i + 1) * TILE)
            after = slice((i + 1) * TILE, (i + 2) * TILE) if i + 1 < tiles else None
            top, slot = one_tile(i, here, after, top, slot)


def attend(kv, queries, states, work, pack=(), after=()):
    sets = len(queries)
    fresh = tuple(n for n, state in enumerate(states) if state is None)
    width = BLOCK - TILE * len(pack)
    out_shape = [jax.ShapeDtypeStruct((PACK_ROWS, TILE), jnp.bfloat16)] * len(pack)
    if width > 0:
        out_shape += [
            jax.ShapeDtypeStruct((1, width), jnp.float32),
            jax.ShapeDtypeStruct((1, width), jnp.float32),
            jax.ShapeDtypeStruct((HEAD_DIM, width), jnp.float32),
        ] * sets
    operands = list(kv) + list(queries)
    for state in states:
        operands += [] if state is None else list(state)
    count = sum(len(chosen) for _, chosen in work)
    return pl.pallas_call(
        functools.partial(
            attend_kernel,
            blocks=len(kv),
            sets=sets,
            work=work,
            fresh=fresh,
            pack=pack,
            waits=len(after),
        ),
        out_shape=tuple(out_shape),
        in_specs=whole(len(operands)) + [pl.BlockSpec(memory_space=pl.ANY)] * len(after),
        out_specs=tuple(whole(len(out_shape))),
        scratch_shapes=[
            pltpu.VMEM((len(kv) * BLOCK, HEAD_DIM), jnp.bfloat16),
            pltpu.VMEM((2, BLOCK, TILE), jnp.float32),
        ],
        compiler_params=params(),
        name="attend",
        cost_estimate=pl.CostEstimate(
            flops=count * 4 * BLOCK * BLOCK * HEAD_DIM * 4,
            bytes_accessed=2**20,
            transcendentals=count * BLOCK * BLOCK,
        ),
    )(*operands, *after)


def unpack(pack_ref):
    split = pack_ref[HEAD_DIM:PACK_ROWS, :].astype(jnp.float32)
    return pack_ref[0:HEAD_DIM, :].astype(jnp.float32), split[0:1] + split[1:2] + split[2:3]


def merge(first, first_lse, second, second_lse):
    top = jnp.maximum(first_lse, second_lse)
    a = jnp.exp2(first_lse - top)
    b = jnp.exp2(second_lse - top)
    inverse = 1.0 / (a + b)
    return (first * (a * inverse) + second * (b * inverse)).astype(jnp.bfloat16)


def output_kernel(m_ref, l_ref, acc_ref, mine_ref, core_ref, diagonal_ref, w_ref, *out_refs):
    total = l_ref[...]
    here = merge(
        acc_ref[...] / total, m_ref[...] * SCORE_SCALE + jnp.log2(total), *unpack(mine_ref)
    )
    other = merge(*unpack(core_ref), *unpack(diagonal_ref))
    attended = jnp.concatenate([here, other], axis=0).T
    width = out_refs[0].shape[1]
    for n, out_ref in enumerate(out_refs):
        out_ref[...] = jnp.dot(
            attended,
            w_ref[:, n * width : (n + 1) * width],
            preferred_element_type=jnp.float32,
        ).astype(jnp.bfloat16)


def output(state, mine, core, diagonal, w_out):
    shape = jax.ShapeDtypeStruct((HALF, FEATURES // len(STEPS)), jnp.bfloat16)
    return pl.pallas_call(
        output_kernel,
        out_shape=(shape,) * len(STEPS),
        in_specs=whole(7),
        out_specs=tuple(whole(len(STEPS))),
        compiler_params=params(),
        name="output_project",
    )(*state, mine, core, diagonal, w_out)


def add_kernel(*refs, terms):
    total = refs[0][...].astype(jnp.float32)
    for ref in refs[1:terms]:
        total = total + ref[...].astype(jnp.float32)
    refs[-1][...] = total.astype(jnp.bfloat16)


def add(*terms, after=()):
    return pl.pallas_call(
        functools.partial(add_kernel, terms=len(terms)),
        out_shape=jax.ShapeDtypeStruct(terms[0].shape, jnp.bfloat16),
        in_specs=whole(len(terms)) + [pl.BlockSpec(memory_space=pl.ANY)] * len(after),
        out_specs=whole(1)[0],
        compiler_params=params(),
        name="add",
    )(*terms, *after)


def finish_kernel(tokens_ref, scale_ref, *refs):
    out_ref = refs[-1]
    total = refs[0][...].astype(jnp.float32)
    for part_ref in refs[1:-1]:
        total = total + part_ref[...].astype(jnp.float32)
    scale = scale_ref[0:1, :]
    out_ref[...] = (tokens_ref[...].astype(jnp.float32) + scale * total).astype(jnp.bfloat16)


def finish(parts, tokens, scale):
    return pl.pallas_call(
        finish_kernel,
        out_shape=jax.ShapeDtypeStruct(tokens.shape, jnp.bfloat16),
        in_specs=whole(2 + len(parts)),
        out_specs=whole(1)[0],
        compiler_params=params(),
        name="finish",
    )(tokens, scale, *parts)


def per_device(tokens, norm_gain, norm_bias, w_query, w_key, w_value, w_out, layer_scale):
    groups = lax.axis_size("heads")
    width = FEATURES // groups
    core = lax.axis_index("frames") % CORE
    x, y = lax.axis_index("heads") // Y_LO, lax.axis_index("heads") % Y_LO
    sources = [((x - dx) % X) * Y_LO + (y ^ dy) for dx, dy in STEPS]
    targets = [((x + dx) % X) * Y_LO + (y ^ dy) for dx, dy in STEPS]
    place = jnp.stack([core, *sources, *targets]).astype(jnp.int32)

    across = send_heads(tokens, (2, 0))
    beside = send_heads(tokens, (0, 1))
    blocks = [tokens, beside, send_heads(tokens, (1, 0)), send_heads(tokens, (3, 0)), across]
    blocks += [send_heads(beside, (1, 0)), send_heads(beside, (3, 0)), send_heads(across, (0, 1))]
    w_all, vectors = prepare(
        place,
        w_query,
        w_key,
        w_value,
        norm_gain.reshape(groups, width),
        norm_bias.reshape(groups, width),
    )
    keep, give = project(blocks, vectors, w_all)
    queries, own = join(keep, send(give, 0, 0, 1))
    w_last, scale = arrange(place, w_out, layer_scale.reshape(1, width), own)
    right, left = own, own
    mine, theirs = None, None
    for step in range(4):
        near = (right, left)
        if step == 2:
            right, _ = lax.optimization_barrier((right, mine[0]))
            left, _ = lax.optimization_barrier((left, mine[0]))
        right = send(right, 0, 1, 0)
        if step < 3:
            left = send(left, 0, -1, 0)
        if step == 0:
            partner = send(queries, 1, 0, 0)
            mine = attend([own], [queries], [None], ((0, (0,)),))
        elif step == 1:
            late = near[1]
            both = attend(
                [own, *near],
                [queries, partner],
                [mine, theirs],
                ((1, (0, 1, 2)), (0, (1,))),
                after=[w_last],
            )
            mine, theirs = both[:3], both[3:]
        elif step == 2:
            both = attend(near, [queries, partner], [mine, theirs], ((0, (0, 1)), (1, (0,))))
            mine, theirs = both[:3], both[3:]
            theirs = attend(near[1:], [partner], [theirs], ((0, (0,)),), after=[right])
        else:
            both = attend(near, [queries, partner], [mine, theirs], ((0, (0, 1)), (1, (0, 1))))
            mine, theirs = both[:3], both[3:]
    for_mine, for_other = attend([right], [partner], [theirs], ((0, (0,)),), pack=(0, 1))
    from_partner = send(for_mine, 1, 0, 0)
    from_diagonal = send(for_other, 1, 0, 1)
    for_core, *state = attend(
        [late, right], [queries], [mine], ((0, (0, 1)),), pack=(1,)
    )
    from_core = send(for_core, 0, 0, 1)
    terms = dict(zip(STEPS, output(state, from_partner, from_core, from_diagonal, w_last)))
    by_column = [send_heads(terms[1, 1], (1, 0)), send_heads(terms[3, 1], (3, 0))]
    parts = [send_heads(add(terms[0, 1], *by_column), (0, 1))]
    by_partner = send_heads(terms[2, 1], (0, 1))
    parts += [send_heads(add(terms[2, 0], by_partner), (2, 0))]
    parts += [send_heads(terms[1, 0], (1, 0)), send_heads(terms[3, 0], (3, 0)), terms[0, 0]]
    return finish(parts, tokens, scale)


def solution(mesh):
    in_specs = (
        P("frames", "heads"),
        P(),
        P(),
        P(None, "heads"),
        P(None, "heads"),
        P(None, "heads"),
        P("heads", None),
        P("heads"),
    )
    out_specs = P("frames", "heads")
    return jax.shard_map(
        per_device, mesh=mesh, in_specs=in_specs, out_specs=out_specs, check_vma=False
    )
```

```python
import functools

import jax
import jax.numpy as jnp
from jax import lax
from jax.experimental import pallas as pl
from jax.experimental.pallas import tpu as pltpu
from jax.sharding import PartitionSpec as P

HEAD_DIM = 64
HALF = 512
BLOCK = 1024
TILE = 512
FEATURES = 1024
LOG2E = 1.4426950408889634
SCORE_SCALE = HEAD_DIM ** (-0.5) * LOG2E
PACK_ROWS = 80

Y_HI, Z, CORE = 2, 8, 2


def frames_shift(dy, dz, dc):
    pairs = []
    for y in range(Y_HI):
        for z in range(Z):
            for c in range(CORE):
                source = (y * Z + z) * CORE + c
                target = ((y ^ dy) * Z + (z + dz) % Z) * CORE + (c ^ dc)
                pairs.append((source, target))
    return pairs


def send(array, dy, dz, dc):
    return lax.ppermute(array, "frames", frames_shift(dy, dz, dc))


X, Y_LO = 4, 2
STEPS = ((0, 0), (0, 1), (1, 0), (3, 0), (2, 0), (1, 1), (3, 1), (2, 1))


def heads_shift(dx, dy):
    return [
        (x * Y_LO + y, ((x + dx) % X) * Y_LO + (y ^ dy)) for x in range(X) for y in range(Y_LO)
    ]


def send_heads(array, step):
    return lax.ppermute(array, "heads", heads_shift(*step))


def params(limit=48):
    return pltpu.CompilerParams(vmem_limit_bytes=limit * 2**20)


def whole(count):
    return [pl.BlockSpec(memory_space=pltpu.VMEM)] * count


def prepare_kernel(
    place_ref, wq_hbm, wk_hbm, wv_hbm, gain_hbm, bias_hbm,
    w_ref, vectors_ref,
    wq_ref, wk_ref, wv_ref, gain_ref, bias_ref, flipped_ref, done,
):
    pairs = (
        (wq_hbm, wq_ref), (wk_hbm, wk_ref), (wv_hbm, wv_ref),
        (gain_hbm, gain_ref), (bias_hbm, bias_ref),
    )
    copies = [pltpu.make_async_copy(a, b, done.at[n]) for n, (a, b) in enumerate(pairs)]
    for copy in copies:
        copy.start()
    for copy in copies:
        copy.wait()
    core = place_ref[0]
    heads = [pl.ds(pl.multiple_of(h * HEAD_DIM, HEAD_DIM), HEAD_DIM) for h in (core, 1 - core)]
    count = len(STEPS)
    width = FEATURES // count

    def columns(n):
        return pl.ds(pl.multiple_of(place_ref[n] * width, width), width)

    for k, ref in enumerate((wq_ref, wk_ref, wv_ref)):
        flipped_ref[...] = ref[...].T
        for h, rows in enumerate(heads):
            at = (3 * h + k) * HEAD_DIM
            for n in range(count):
                w_ref[at : at + HEAD_DIM, n * width : (n + 1) * width] = flipped_ref[
                    rows, columns(1 + n)
                ]
    for n in range(count):
        j = place_ref[1 + n]
        vectors_ref[n : n + 1, :] = gain_ref[pl.ds(j, 1), :]
        vectors_ref[count + n : count + n + 1, :] = bias_ref[pl.ds(j, 1), :]


def prepare(place, wq, wk, wv, gain, bias):
    return pl.pallas_call(
        prepare_kernel,
        out_shape=(
            jax.ShapeDtypeStruct((6 * HEAD_DIM, FEATURES), jnp.bfloat16),
            jax.ShapeDtypeStruct((2 * len(STEPS), FEATURES // len(STEPS)), jnp.float32),
        ),
        in_specs=[pl.BlockSpec(memory_space=pltpu.SMEM)]
        + [pl.BlockSpec(memory_space=pltpu.MemorySpace.HBM)] * 5,
        out_specs=tuple(whole(2)),
        scratch_shapes=[pltpu.VMEM(a.shape, a.dtype) for a in (wq, wk, wv, gain, bias)]
        + [pltpu.VMEM((2 * HEAD_DIM, FEATURES), jnp.bfloat16), pltpu.SemaphoreType.DMA((5,))],
        compiler_params=params(),
        name="prepare",
        cost_estimate=pl.CostEstimate(
            flops=2 * HALF * FEATURES * 384, bytes_accessed=4 * 2**20, transcendentals=0
        ),
    )(place, wq, wk, wv, gain, bias)


def arrange_kernel(place_ref, w_ref, scale_ref, after_ref, out_ref, vector_ref):
    core = place_ref[0]
    count = len(STEPS)
    width = FEATURES // count
    for at, h in enumerate((core, 1 - core)):
        rows = pl.ds(pl.multiple_of(h * HEAD_DIM, HEAD_DIM), HEAD_DIM)
        for n in range(count):
            columns = pl.ds(pl.multiple_of(place_ref[1 + count + n] * width, width), width)
            out_ref[at * HEAD_DIM : (at + 1) * HEAD_DIM, n * width : (n + 1) * width] = w_ref[
                rows, columns
            ]
    vector_ref[...] = jnp.broadcast_to(scale_ref[...], vector_ref.shape)


def arrange(place, w_out, scale, after):
    return pl.pallas_call(
        arrange_kernel,
        out_shape=(
            jax.ShapeDtypeStruct(w_out.shape, w_out.dtype),
            jax.ShapeDtypeStruct((8, scale.shape[1]), jnp.float32),
        ),
        in_specs=[pl.BlockSpec(memory_space=pltpu.SMEM)]
        + whole(2)
        + [pl.BlockSpec(memory_space=pl.ANY)],
        out_specs=tuple(whole(2)),
        compiler_params=params(),
        name="arrange",
    )(place, w_out, scale, after)


def project_kernel(*refs):
    x_refs = refs[:8]
    vectors_ref, w_ref, keep, give, normed_ref = refs[8:]
    count = len(x_refs)
    width = x_refs[0].shape[1]
    total = jnp.zeros((HALF, width), jnp.float32)
    for x_ref in x_refs:
        total = total + x_ref[...].astype(jnp.float32)
    mean = jnp.sum(total, axis=1, keepdims=True) * (1.0 / FEATURES)
    squares = jnp.zeros((HALF, width), jnp.float32)
    for x_ref in x_refs:
        centred = x_ref[...].astype(jnp.float32) - mean
        squares = squares + centred * centred
    variance = jnp.sum(squares, axis=1, keepdims=True) * (1.0 / FEATURES)
    inverse = lax.rsqrt(variance + 1e-06)
    for n, x_ref in enumerate(x_refs):
        centred = x_ref[...].astype(jnp.float32) - mean
        gain = vectors_ref[n : n + 1, :]
        bias = vectors_ref[count + n : count + n + 1, :]
        normed = centred * inverse * gain + bias
        normed_ref[:, n * width : (n + 1) * width] = normed.astype(jnp.bfloat16)
    for h, out in enumerate((keep, give)):
        out[...] = lax.dot_general(
            w_ref[h * 3 * HEAD_DIM : (h + 1) * 3 * HEAD_DIM, :],
            normed_ref[...],
            (((1,), (1,)), ((), ())),
            preferred_element_type=jnp.float32,
        ).astype(jnp.bfloat16)


def project(blocks, vectors, w):
    shape = jax.ShapeDtypeStruct((3 * HEAD_DIM, HALF), jnp.bfloat16)
    return pl.pallas_call(
        project_kernel,
        out_shape=(shape, shape),
        in_specs=whole(10),
        out_specs=tuple(whole(2)),
        scratch_shapes=[pltpu.VMEM((HALF, FEATURES), jnp.bfloat16)],
        compiler_params=params(),
        name="norm_project",
        cost_estimate=pl.CostEstimate(
            flops=2 * HALF * FEATURES * 384, bytes_accessed=2 * 2**20, transcendentals=HALF
        ),
    )(*blocks, vectors, w)


def join_kernel(keep, taken, q_ref, kv_ref):
    for ref, columns in ((keep, slice(0, HALF)), (taken, slice(HALF, 2 * HALF))):
        q_ref[:, columns] = ref[0:HEAD_DIM, :]
        kv_ref[:, columns] = ref[HEAD_DIM:, :]


def join(keep, taken):
    return pl.pallas_call(
        join_kernel,
        out_shape=(
            jax.ShapeDtypeStruct((HEAD_DIM, 2 * HALF), jnp.bfloat16),
            jax.ShapeDtypeStruct((2 * HEAD_DIM, 2 * HALF), jnp.bfloat16),
        ),
        in_specs=whole(2),
        out_specs=tuple(whole(2)),
        compiler_params=params(),
        name="join",
    )(keep, taken)


def attend_kernel(*refs, blocks, sets, work, fresh, pack, waits):
    kv = refs[:blocks]
    queries = refs[blocks : blocks + sets]
    at = blocks + sets
    old = {}
    for which in range(sets):
        if which not in fresh:
            old[which] = refs[at : at + 3]
            at += 3
    k_ref, s_ref = refs[-2:]
    at += waits
    packs, new = refs[at : at + len(pack)], refs[at + len(pack) : -2]
    for b in range(blocks):
        k_ref[b * BLOCK : (b + 1) * BLOCK, :] = kv[b][0:HEAD_DIM, :].T

    steps = [
        (which, b, n == 0, n == len(chosen) - 1)
        for which, chosen in work
        for n, b in enumerate(chosen)
    ]
    tiles = BLOCK // TILE

    def score(step, columns, slot):
        which, b = step[:2]
        s = jnp.dot(
            k_ref[b * BLOCK : (b + 1) * BLOCK, :],
            queries[which][:, columns],
            preferred_element_type=jnp.float32,
        )
        s_ref[slot] = s
        return jnp.max(s, axis=0, keepdims=True)

    def one_tile(tile, columns, next_columns, top, slot):
        for n, (which, b, first, last) in enumerate(steps):
            if first:
                if which in fresh:
                    m = jnp.full((1, TILE), -jnp.inf, jnp.float32)
                    l = jnp.zeros((1, TILE), jnp.float32)
                    acc = jnp.zeros((HEAD_DIM, TILE), jnp.float32)
                else:
                    m, l, acc = (ref[:, columns] for ref in old[which])
            newest = jnp.maximum(m, top)
            factor = jnp.exp2((m - newest) * SCORE_SCALE)
            if n + 1 < len(steps):
                top = score(steps[n + 1], columns, 1 - slot)
            elif next_columns is not None:
                top = score(steps[0], next_columns, 1 - slot)
            weights = jnp.exp2((s_ref[slot] - newest) * SCORE_SCALE)
            slot = 1 - slot
            l = l * factor + jnp.sum(weights, axis=0, keepdims=True)
            acc = acc * factor + jnp.dot(
                kv[b][HEAD_DIM:, :],
                weights.astype(jnp.bfloat16),
                preferred_element_type=jnp.float32,
            )
            m = newest
            if last and tile not in pack:
                new[3 * which][:, columns] = m
                new[3 * which + 1][:, columns] = l
                new[3 * which + 2][:, columns] = acc
            elif last:
                pack_ref = packs[pack.index(tile)]
                pack_ref[0:HEAD_DIM, :] = (acc / l).astype(jnp.bfloat16)
                lse = m * SCORE_SCALE + jnp.log2(l)
                high = lse.astype(jnp.bfloat16).astype(jnp.float32)
                middle = (lse - high).astype(jnp.bfloat16).astype(jnp.float32)
                low = lse - high - middle
                row = lax.broadcasted_iota(jnp.int32, (PACK_ROWS - HEAD_DIM, TILE), 0)
                rows = jnp.where(row == 0, high, jnp.where(row == 1, middle, low))
                pack_ref[HEAD_DIM:PACK_ROWS, :] = rows.astype(jnp.bfloat16)
        return top, slot

    if len(steps) % 2 == 0 and not pack:

        def body(i, top):
            here = pl.ds(pl.multiple_of(i * TILE, TILE), TILE)
            after = pl.ds(pl.multiple_of(lax.rem(i + 1, tiles) * TILE, TILE), TILE)
            return one_tile(-1, here, after, top, 0)[0]

        lax.fori_loop(0, tiles, body, score(steps[0], slice(0, TILE), 0))
    else:
        top, slot = score(steps[0], slice(0, TILE), 0), 0
        for i in range(tiles):
            here = slice(i * TILE, (i + 1) * TILE)
            after = slice((i + 1) * TILE, (i + 2) * TILE) if i + 1 < tiles else None
            top, slot = one_tile(i, here, after, top, slot)


def attend(kv, queries, states, work, pack=(), after=()):
    sets = len(queries)
    fresh = tuple(n for n, state in enumerate(states) if state is None)
    width = BLOCK - TILE * len(pack)
    out_shape = [jax.ShapeDtypeStruct((PACK_ROWS, TILE), jnp.bfloat16)] * len(pack)
    if width > 0:
        out_shape += [
            jax.ShapeDtypeStruct((1, width), jnp.float32),
            jax.ShapeDtypeStruct((1, width), jnp.float32),
            jax.ShapeDtypeStruct((HEAD_DIM, width), jnp.float32),
        ] * sets
    operands = list(kv) + list(queries)
    for state in states:
        operands += [] if state is None else list(state)
    count = sum(len(chosen) for _, chosen in work)
    return pl.pallas_call(
        functools.partial(
            attend_kernel,
            blocks=len(kv),
            sets=sets,
            work=work,
            fresh=fresh,
            pack=pack,
            waits=len(after),
        ),
        out_shape=tuple(out_shape),
        in_specs=whole(len(operands)) + [pl.BlockSpec(memory_space=pl.ANY)] * len(after),
        out_specs=tuple(whole(len(out_shape))),
        scratch_shapes=[
            pltpu.VMEM((len(kv) * BLOCK, HEAD_DIM), jnp.bfloat16),
            pltpu.VMEM((2, BLOCK, TILE), jnp.float32),
        ],
        compiler_params=params(),
        name="attend",
        cost_estimate=pl.CostEstimate(
            flops=count * 4 * BLOCK * BLOCK * HEAD_DIM * 4,
            bytes_accessed=2**20,
            transcendentals=count * BLOCK * BLOCK,
        ),
    )(*operands, *after)


def unpack(pack_ref):
    split = pack_ref[HEAD_DIM:PACK_ROWS, :].astype(jnp.float32)
    return pack_ref[0:HEAD_DIM, :].astype(jnp.float32), split[0:1] + split[1:2] + split[2:3]


def merge(first, first_lse, second, second_lse):
    top = jnp.maximum(first_lse, second_lse)
    a = jnp.exp2(first_lse - top)
    b = jnp.exp2(second_lse - top)
    inverse = 1.0 / (a + b)
    return (first * (a * inverse) + second * (b * inverse)).astype(jnp.bfloat16)


def output_kernel(m_ref, l_ref, acc_ref, mine_ref, core_ref, diagonal_ref, w_ref, *out_refs):
    total = l_ref[...]
    here = merge(
        acc_ref[...] / total, m_ref[...] * SCORE_SCALE + jnp.log2(total), *unpack(mine_ref)
    )
    other = merge(*unpack(core_ref), *unpack(diagonal_ref))
    attended = jnp.concatenate([here, other], axis=0).T
    width = out_refs[0].shape[1]
    for n, out_ref in enumerate(out_refs):
        out_ref[...] = jnp.dot(
            attended,
            w_ref[:, n * width : (n + 1) * width],
            preferred_element_type=jnp.float32,
        ).astype(jnp.bfloat16)


def output(state, mine, core, diagonal, w_out):
    shape = jax.ShapeDtypeStruct((HALF, FEATURES // len(STEPS)), jnp.bfloat16)
    return pl.pallas_call(
        output_kernel,
        out_shape=(shape,) * len(STEPS),
        in_specs=whole(7),
        out_specs=tuple(whole(len(STEPS))),
        compiler_params=params(),
        name="output_project",
    )(*state, mine, core, diagonal, w_out)


def add_kernel(*refs, terms):
    total = refs[0][...].astype(jnp.float32)
    for ref in refs[1:terms]:
        total = total + ref[...].astype(jnp.float32)
    refs[-1][...] = total.astype(jnp.bfloat16)


def add(*terms, after=()):
    return pl.pallas_call(
        functools.partial(add_kernel, terms=len(terms)),
        out_shape=jax.ShapeDtypeStruct(terms[0].shape, jnp.bfloat16),
        in_specs=whole(len(terms)) + [pl.BlockSpec(memory_space=pl.ANY)] * len(after),
        out_specs=whole(1)[0],
        compiler_params=params(),
        name="add",
    )(*terms, *after)


def finish_kernel(tokens_ref, scale_ref, *refs):
    out_ref = refs[-1]
    total = refs[0][...].astype(jnp.float32)
    for part_ref in refs[1:-1]:
        total = total + part_ref[...].astype(jnp.float32)
    scale = scale_ref[0:1, :]
    out_ref[...] = (tokens_ref[...].astype(jnp.float32) + scale * total).astype(jnp.bfloat16)


def finish(parts, tokens, scale):
    return pl.pallas_call(
        finish_kernel,
        out_shape=jax.ShapeDtypeStruct(tokens.shape, jnp.bfloat16),
        in_specs=whole(2 + len(parts)),
        out_specs=whole(1)[0],
        compiler_params=params(),
        name="finish",
    )(tokens, scale, *parts)


def per_device(tokens, norm_gain, norm_bias, w_query, w_key, w_value, w_out, layer_scale):
    groups = lax.axis_size("heads")
    width = FEATURES // groups
    core = lax.axis_index("frames") % CORE
    x, y = lax.axis_index("heads") // Y_LO, lax.axis_index("heads") % Y_LO
    sources = [((x - dx) % X) * Y_LO + (y ^ dy) for dx, dy in STEPS]
    targets = [((x + dx) % X) * Y_LO + (y ^ dy) for dx, dy in STEPS]
    place = jnp.stack([core, *sources, *targets]).astype(jnp.int32)

    across = send_heads(tokens, (2, 0))
    beside = send_heads(tokens, (0, 1))
    blocks = [tokens, beside, send_heads(tokens, (1, 0)), send_heads(tokens, (3, 0)), across]
    blocks += [send_heads(beside, (1, 0)), send_heads(beside, (3, 0)), send_heads(across, (0, 1))]
    w_all, vectors = prepare(
        place,
        w_query,
        w_key,
        w_value,
        norm_gain.reshape(groups, width),
        norm_bias.reshape(groups, width),
    )
    keep, give = project(blocks, vectors, w_all)
    queries, own = join(keep, send(give, 0, 0, 1))
    w_last, scale = arrange(place, w_out, layer_scale.reshape(1, width), own)
    right, left = own, own
    mine, theirs = None, None
    for step in range(4):
        near = (right, left)
        if step == 2:
            right, _ = lax.optimization_barrier((right, mine[0]))
            left, _ = lax.optimization_barrier((left, mine[0]))
        right = send(right, 0, 1, 0)
        if step < 3:
            left = send(left, 0, -1, 0)
        if step == 0:
            partner = send(queries, 1, 0, 0)
            mine = attend([own], [queries], [None], ((0, (0,)),))
        elif step == 1:
            late = near[1]
            both = attend(
                [own, *near],
                [queries, partner],
                [mine, theirs],
                ((1, (0, 1, 2)), (0, (1,))),
                after=[w_last],
            )
            mine, theirs = both[:3], both[3:]
        elif step == 2:
            both = attend(near, [queries, partner], [mine, theirs], ((0, (0, 1)), (1, (0,))))
            mine, theirs = both[:3], both[3:]
            theirs = attend(near[1:], [partner], [theirs], ((0, (0,)),), after=[right])
        else:
            both = attend(near, [queries, partner], [mine, theirs], ((0, (0, 1)), (1, (0, 1))))
            mine, theirs = both[:3], both[3:]
    for_mine, for_other = attend([right], [partner], [theirs], ((0, (0,)),), pack=(0, 1))
    from_partner = send(for_mine, 1, 0, 0)
    from_diagonal = send(for_other, 1, 0, 1)
    for_core, *state = attend(
        [late, right], [queries], [mine], ((0, (0, 1)),), pack=(1,)
    )
    from_core = send(for_core, 0, 0, 1)
    terms = dict(zip(STEPS, output(state, from_partner, from_core, from_diagonal, w_last)))
    by_column = [send_heads(terms[1, 1], (1, 0)), send_heads(terms[3, 1], (3, 0))]
    parts = [send_heads(add(terms[0, 1], *by_column), (0, 1))]
    by_partner = send_heads(terms[2, 1], (0, 1))
    parts += [send_heads(add(terms[2, 0], by_partner), (2, 0))]
    parts += [send_heads(terms[1, 0], (1, 0)), send_heads(terms[3, 0], (3, 0)), terms[0, 0]]
    return finish(parts, tokens, scale)


def solution(mesh):
    in_specs = (
        P("frames", "heads"),
        P(),
        P(),
        P(None, "heads"),
        P(None, "heads"),
        P(None, "heads"),
        P("heads", None),
        P("heads"),
    )
    out_specs = P("frames", "heads")
    return jax.shard_map(
        per_device, mesh=mesh, in_specs=in_specs, out_specs=out_specs, check_vma=False
    )
```
